256 devices in a mesh: row: 8 (over z), col: 4 (over y_lo, core), ch: 8 (over x, y_hi).
Axes of the slice: x: 4, y: 4 (y_hi: 2, y_lo: 2; y = y_hi * 2 + y_lo), z: 8, core: 2. Of those that a mesh axis runs over, the one named last changes fastest.
Arguments:
- spectra: float32 [384, 256, 1024], P('ch', 'row', 'col'), may hold values from 0 to 1
- pixel_factor: float32 [64, 256, 1024], P(None, 'row', 'col'), may hold values from 0.1 to 1
- channel_factor: float32 [64, 384], P(None, 'ch'), may hold values from 0.1 to 1
- labels: int32 [256, 1024], P('row', 'col'), may hold values from 0 to 3
Outputs:
- smoothed_factor: float32 [64, 256, 1024], P(None, 'row', 'col')
- new_channel: float32 [64, 384], P(None, 'ch')
The draws below stay inside these ranges and needn't reach their ends.
All inputs are finite; a program needn't handle non-finite values.
Results may differ from the reference program's by a relative error of at most 0.000068.
Values sent between devices are 32-bit elements; how exact they have to be, the bound alone decides.
No kernel may reach another device: no remote copies, remote signals or barrier semaphores. Data moves between devices by JAX's collectives and lax.ppermute only.
A program may use at most 64 MiB of HBM per device.

```python
import math
import jax
import jax.numpy as jnp
from jax import lax

K = 64
C = 384
SMOOTH = 3
IMG_ROWS = 256
IMG_COLS = 1024


def place_ends(values, own_key, low, top_value):
    index_at = [jax.random.randint(jax.random.fold_in(own_key, axis), (), 0, length) for axis, length in enumerate(values.shape)]
    longest = values.shape.index(max(values.shape))
    beside = index_at[:longest] + [(index_at[longest] + 1) % values.shape[longest]] + index_at[longest + 1:]
    return values.at[tuple(index_at)].set(low).at[tuple(beside)].set(top_value)


def shard_levels(own_key, dims, pieces, low, largest):
    level = 1.0
    for position, parts in pieces:
        draws = jax.random.uniform(jax.random.fold_in(jax.random.fold_in(own_key, 6), position), (parts,), jnp.float32, low / len(pieces), largest / len(pieces))
        level = level * jnp.repeat(jnp.exp(draws), dims[position] // parts).reshape((-1,) + (1,) * (len(dims) - 1 - position))
    return level


def setup_inputs(seed: int = 0) -> dict:
    streams_of = jax.random.split(jax.random.key(seed), 5)
    spectra = jnp.clip(1.0 * jax.random.uniform(streams_of[0], (C, IMG_ROWS, IMG_COLS), jnp.float32) ** shard_levels(streams_of[0], (C, IMG_ROWS, IMG_COLS), ((0, 8), (1, 8), (2, 4)), -0.2, 0.2), 0.0, 1.0)
    pixel_factor = jnp.clip(jnp.exp(math.log(1.0) - 2.3025851 * jax.random.uniform(streams_of[1], (K, IMG_ROWS, IMG_COLS), jnp.float32) ** shard_levels(streams_of[1], (K, IMG_ROWS, IMG_COLS), ((1, 8), (2, 4)), -0.2, 0.2)), 0.1, 1.0)
    channel_factor = jnp.clip(jnp.exp(math.log(1.0) - 2.3025851 * jax.random.uniform(streams_of[2], (K, C), jnp.float32) ** shard_levels(streams_of[2], (K, C), ((1, 8),), -0.2, 0.2)), 0.1, 1.0)
    labels = place_ends(jax.random.randint(streams_of[3], (IMG_ROWS, IMG_COLS), 0, 4), jax.random.fold_in(streams_of[3], 1), 0, 3).astype(jnp.int32)
    return dict(spectra=spectra, pixel_factor=pixel_factor, channel_factor=channel_factor, labels=labels)


epsilon = 1e-9


def coefficients(marked):
    center = marked[1:-1, 1:-1]
    result = []
    for neighbour in (marked[:-2, 1:-1], marked[2:, 1:-1], marked[1:-1, :-2], marked[1:-1, 2:]):
        result.append(jnp.where(neighbour == 0, 0.0, jnp.where(neighbour == center, 1.0, 0.25)).astype(jnp.float32))
    return result


def smooth_once(padded, field, weights):
    combined = field + weights[0] * padded[:, :-2, 1:-1] + weights[1] * padded[:, 2:, 1:-1]
    combined = combined + weights[2] * padded[:, 1:-1, :-2] + weights[3] * padded[:, 1:-1, 2:]
    return combined / (1.0 + weights[0] + weights[1] + weights[2] + weights[3])


def reference(spectra, pixel_factor, channel_factor, labels):
    precise = lax.Precision.HIGHEST
    contraction = (((1,), (1,)), ((), ()))
    factor_rank = pixel_factor.shape[0]
    flat_pixel = pixel_factor.reshape(factor_rank, -1)
    flat_data = spectra.reshape(spectra.shape[0], -1)
    chan_top = lax.dot_general(flat_pixel, flat_data, contraction, precision=precise, preferred_element_type=jnp.float32)
    pixel_gram = lax.dot_general(flat_pixel, flat_pixel, contraction, precision=precise, preferred_element_type=jnp.float32)
    new_channel = channel_factor * chan_top / (jnp.dot(pixel_gram, channel_factor, precision=precise, preferred_element_type=jnp.float32) + epsilon)
    pixel_top = jnp.dot(new_channel, flat_data, precision=precise, preferred_element_type=jnp.float32)
    chan_gram = lax.dot_general(new_channel, new_channel, contraction, precision=precise, preferred_element_type=jnp.float32)
    lower = jnp.dot(chan_gram, flat_pixel, precision=precise, preferred_element_type=jnp.float32)
    raised = (flat_pixel * pixel_top / (lower + epsilon)).reshape(pixel_factor.shape)
    marked = jnp.pad(labels + 1, 1)
    weights = coefficients(marked)
    field = raised
    for iteration in range(SMOOTH):
        padded = jnp.pad(field, ((0, 0), (1, 1), (1, 1)))
        field = smooth_once(padded, field, weights)
    return field, new_channel
```

```python
import jax
import jax.numpy as jnp
from jax import lax
from jax.sharding import PartitionSpec as P

SMOOTH = 3
epsilon = 1e-09


def with_borders(block, sides, width):
    for axis, dim in sides:
        count = lax.axis_size(axis)
        forward = [(i, i + 1) for i in range(count - 1)]
        backward = [(target, source) for source, target in forward]
        low = lax.ppermute(
            lax.slice_in_dim(block, block.shape[dim] - width, None, axis=dim), axis, forward
        )
        high = lax.ppermute(lax.slice_in_dim(block, 0, width, axis=dim), axis, backward)
        block = jnp.concatenate([low, block, high], axis=dim)
    return block


def coefficients(marked):
    center = marked[1:-1, 1:-1]
    result = []
    for neighbour in (marked[:-2, 1:-1], marked[2:, 1:-1], marked[1:-1, :-2], marked[1:-1, 2:]):
        result.append(
            jnp.where(neighbour == 0, 0.0, jnp.where(neighbour == center, 1.0, 0.25)).astype(
                jnp.float32
            )
        )
    return result


def trimmed(array, width):
    return array if width == 0 else array[..., width:-width, width:-width]


def smooth_share(field, weights):
    for step in range(SMOOTH):
        up, down, left, right = (trimmed(weight, step) for weight in weights)
        combined = field[:, 1:-1, 1:-1] + up * field[:, :-2, 1:-1] + down * field[:, 2:, 1:-1]
        combined = combined + left * field[:, 1:-1, :-2] + right * field[:, 1:-1, 2:]
        field = combined / (1.0 + up + down + left + right)
    return field


def doubled_sum(value, axis):
    count = lax.axis_size(axis)
    distance = 1
    while distance < count:
        value = value + lax.ppermute(value, axis, [(i, i ^ distance) for i in range(count)])
        distance *= 2
    return value


def copies_of_all(value, axis):
    count = lax.axis_size(axis)
    copies = jnp.broadcast_to(value[None], (count,) + value.shape)
    return lax.all_to_all(copies, axis, 0, 0, tiled=True)


def shards(spectra, pixel_factor, channel_factor, labels):
    precise = lax.Precision.HIGHEST
    contraction = (((1,), (1,)), ((), ()))
    factor_rank, row_count, col_count = pixel_factor.shape
    pixels = row_count * col_count
    channels = spectra.shape[0]
    shares = lax.axis_size("ch")
    share = factor_rank // shares
    flat_pixel = pixel_factor.reshape(factor_rank, pixels)
    flat_data = spectra.reshape(channels, pixels)
    marks = with_borders(labels + 1, (("row", 0), ("col", 1)), SMOOTH)
    weights = coefficients(marks)
    chan_top = lax.dot_general(
        flat_pixel, flat_data, contraction, precision=precise, preferred_element_type=jnp.float32
    )
    pixel_gram = lax.dot_general(
        flat_pixel, flat_pixel, contraction, precision=precise, preferred_element_type=jnp.float32
    )
    sums = doubled_sum(jnp.concatenate([pixel_gram, chan_top], axis=1), "col")
    sums = copies_of_all(sums, "row").sum(axis=0)
    pixel_gram, chan_top = sums[:, :factor_rank], sums[:, factor_rank:]
    lower = jnp.dot(
        pixel_gram, channel_factor, precision=precise, preferred_element_type=jnp.float32
    )
    new_channel = channel_factor * chan_top / (lower + epsilon)
    part_top = jnp.dot(
        new_channel, flat_data, precision=precise, preferred_element_type=jnp.float32
    )
    part_gram = lax.dot_general(
        new_channel, new_channel, contraction, precision=precise, preferred_element_type=jnp.float32
    )
    parts = jnp.concatenate([part_top, jnp.pad(part_gram, ((0, 0), (0, -factor_rank % 128)))], 1)
    parts = parts.reshape(shares, share, -1)
    parts = lax.all_to_all(parts, "ch", 0, 0, tiled=True).sum(axis=0)
    top, gram = parts[:, :pixels], parts[:, pixels : pixels + factor_rank]
    own = lax.dynamic_slice_in_dim(flat_pixel, lax.axis_index("ch") * share, share, axis=0)
    lower = jnp.dot(gram, flat_pixel, precision=precise, preferred_element_type=jnp.float32)
    field = (own * top / (lower + epsilon)).reshape(share, row_count, col_count)
    field = with_borders(field, (("row", 1), ("col", 2)), SMOOTH)
    field = smooth_share(field, weights)
    field = copies_of_all(field, "ch").reshape(factor_rank, row_count, col_count)
    return (field, new_channel)


def solution(mesh):
    placed = (P("ch", "row", "col"), P(None, "row", "col"), P(None, "ch"), P("row", "col"))
    return jax.shard_map(
        shards,
        mesh=mesh,
        in_specs=placed,
        out_specs=(P(None, "row", "col"), P(None, "ch")),
        check_vma=False,
    )
```

```python
import jax
import jax.numpy as jnp
from jax import lax
from jax.experimental import pallas as pl
from jax.experimental.pallas import tpu as pltpu
from jax.sharding import PartitionSpec as P

SMOOTH = 3
LANES = 128
epsilon = 1e-09
VMEM_LIMIT = 56 * 1024 * 1024


def with_borders(block, sides, width):
    for axis, dim in sides:
        count = lax.axis_size(axis)
        forward = [(i, i + 1) for i in range(count - 1)]
        backward = [(target, source) for source, target in forward]
        low = lax.ppermute(
            lax.slice_in_dim(block, block.shape[dim] - width, None, axis=dim), axis, forward
        )
        high = lax.ppermute(lax.slice_in_dim(block, 0, width, axis=dim), axis, backward)
        block = jnp.concatenate([low, block, high], axis=dim)
    return block


def doubled_sum(value, axis):
    count = lax.axis_size(axis)
    distance = 1
    while distance < count:
        value = value + lax.ppermute(value, axis, [(i, i ^ distance) for i in range(count)])
        distance *= 2
    return value


def copies_of_all(value, axis):
    count = lax.axis_size(axis)
    copies = jnp.broadcast_to(value[None], (count,) + value.shape)
    return lax.all_to_all(copies, axis, 0, 0, tiled=True)


def kernel_call(kernel, out_shape, scratch_shapes=(), smem=0, operands=(), flops=0):
    traffic = sum(x.size * 4 for x in operands) + sum(x.size * 4 for x in jax.tree.leaves(out_shape))
    in_specs = [
        pl.BlockSpec(memory_space=pltpu.SMEM if i < smem else pltpu.VMEM)
        for i in range(len(operands))
    ]
    return pl.pallas_call(
        kernel,
        out_shape=out_shape,
        in_specs=in_specs,
        out_specs=jax.tree.map(lambda _: pl.BlockSpec(memory_space=pltpu.VMEM), out_shape),
        scratch_shapes=scratch_shapes,
        compiler_params=pltpu.CompilerParams(vmem_limit_bytes=VMEM_LIMIT),
        cost_estimate=pl.CostEstimate(flops=flops, bytes_accessed=traffic, transcendentals=0),
    )(*operands)


def split(value):
    high = value.astype(jnp.bfloat16)
    low = (value - high.astype(jnp.float32)).astype(jnp.bfloat16)
    return high, low


def gram_kernel(place_ref, data_ref, factor_ref, sums_ref, send_ref, own_ref, rows_ref, wide, tall):
    channels, row_count, col_count = data_ref.shape
    rank = factor_ref.shape[0]
    half = 2 * rank
    for top in (0, half):
        wide[top + rank + channels : top + half, :] = jnp.zeros(
            (rank - channels, row_count * col_count), jnp.bfloat16
        )
    lane = lax.broadcasted_iota(jnp.int32, (rank, LANES), 1)
    data_sides = [jnp.zeros((channels, LANES), jnp.float32)] * 2
    factor_sides = [jnp.zeros((rank, LANES), jnp.float32)] * 2
    for row in range(row_count):
        columns = slice(row * col_count, (row + 1) * col_count)
        data = data_ref[:, row, :]
        factor = factor_ref[:, row, :]
        send_ref[row // 4, row % 4] = data
        rows_ref[row // 4, row % 4] = factor
        if row >= row_count - 3:
            send_ref[row - row_count + 3, 4] = data
            rows_ref[row - row_count + 3, 4] = factor
        if row < 3:
            send_ref[3 + row, 4] = data
            rows_ref[3 + row, 4] = factor
        here = (lane >= 3 * row) & (lane < 3 * row + 3)
        for side, (first, shift) in enumerate(((col_count - LANES, 3 * row + 3), (0, 3 * row))):
            piece = pltpu.roll(data[:, first : first + LANES], shift, 1)
            data_sides[side] = jnp.where(here[:channels], piece, data_sides[side])
            piece = pltpu.roll(factor[:, first : first + LANES], shift, 1)
            factor_sides[side] = jnp.where(here, piece, factor_sides[side])
        high, low = split(factor)
        tall[0:rank, columns] = high
        tall[rank:half, columns] = low
        wide[0:rank, columns] = high
        wide[half : half + rank, columns] = low
        high, low = split(data)
        wide[rank : rank + channels, columns] = high
        wide[half + rank : half + rank + channels, columns] = low
    for side in range(2):
        send_ref[6 + side, 4, :, 0:LANES] = data_sides[side]
        send_ref[6 + side, 4, :, LANES:] = jnp.zeros((channels, col_count - LANES), jnp.float32)
        rows_ref[6 + side, 4, :, 0:LANES] = factor_sides[side]
        rows_ref[6 + side, 4, :, LANES:] = jnp.zeros((rank, col_count - LANES), jnp.float32)
    own_ref[...] = rows_ref[place_ref[0]]
    products = lax.dot_general(
        wide[...], tall[...], (((1,), (1,)), ((), ())), preferred_element_type=jnp.float32
    )
    products = products[0:half] + products[half:]
    products = products + pltpu.roll(products, rank, 1)
    packed = (rank + channels) // 2
    sums_ref[...] = jnp.where(lane[:packed] < rank, products[0:packed], products[packed : 2 * packed])


def channel_kernel(sums_ref, factor_ref, new_ref, copies_ref):
    channels, rank = factor_ref.shape
    total = sums_ref[0]
    for i in range(1, sums_ref.shape[0]):
        total = total + sums_ref[i]
    total = jnp.concatenate([total, pltpu.roll(total, rank, 1)], axis=0)[:, :rank]
    gram, top = total[:rank], total[rank:]
    factor = factor_ref[...]
    lower = lax.dot_general(
        factor,
        gram,
        (((1,), (1,)), ((), ())),
        precision=lax.Precision.HIGHEST,
        preferred_element_type=jnp.float32,
    )
    new = factor * top / (lower + epsilon)
    new_ref[...] = new
    packed = channels // 2
    new = jnp.concatenate([new[:packed], new[packed:]], axis=1)
    for i in range(copies_ref.shape[0]):
        copies_ref[i] = new


def raise_kernel(new_ref, data_ref, factor_ref, raised_ref):
    shares, packed, _ = new_ref.shape
    strip, rank, col_count = factor_ref.shape
    parts = []
    for i in range(shares):
        parts += [new_ref[i], pltpu.roll(new_ref[i], rank, 1)]
    new = jnp.concatenate(parts, axis=0)
    new = jnp.transpose(new)[:rank]
    gram = lax.dot_general(
        new,
        new,
        (((1,), (1,)), ((), ())),
        precision=lax.Precision.HIGHEST,
        preferred_element_type=jnp.float32,
    )
    new = jnp.concatenate(split(new), axis=0)
    gram = jnp.concatenate(split(gram), axis=0)

    def product(left, right):
        high, low = split(right)
        both = jnp.dot(left, high, preferred_element_type=jnp.float32)
        both = both + jnp.dot(left, low, preferred_element_type=jnp.float32)
        return both[:rank] + both[rank:]

    for row in range(strip):
        data = jnp.concatenate([data_ref[i, row] for i in range(shares)], axis=0)
        factor = factor_ref[row]
        raised_ref[row] = factor * product(new, data) / (product(gram, factor) + epsilon)


def smooth_kernel(marks_ref, gathered_ref, out_ref, first, second, weights_ref):
    rank, row_count, col_count = out_ref.shape
    width = marks_ref.shape[1]
    tall = row_count + 2 * SMOOTH
    marks = marks_ref[...]
    total = jnp.ones(marks.shape, jnp.float32)
    found = []
    for shift, axis in ((1, 0), (marks.shape[0] - 1, 0), (1, 1), (width - 1, 1)):
        neighbour = pltpu.roll(marks, shift, axis)
        weight = jnp.where(neighbour == marks, 1.0, 0.25)
        weight = jnp.where(neighbour == 0.0, 0.0, weight)
        found.append(weight)
        total = total + weight
    weights_ref[0] = 1.0 / total
    for i, weight in enumerate(found):
        weights_ref[1 + i] = weight / total
    lane = lax.broadcasted_iota(jnp.int32, (rank, LANES), 1)
    for row in range(tall):
        inner = row - SMOOTH
        if inner < 0:
            main, start, at = gathered_ref[row, 4], LANES, 3 * (row_count + inner)
        elif inner < row_count:
            main, start, at = gathered_ref[inner // 4, inner % 4], 0, 3 * inner
        else:
            main, start, at = gathered_ref[3 + inner - row_count, 4], LANES, 3 * (inner - row_count)
        left = pltpu.roll(gathered_ref[6, 4, :, start : start + LANES], (LANES - 3 - at) % LANES, 1)
        right = pltpu.roll(gathered_ref[7, 4, :, start : start + LANES], (LANES - at) % LANES, 1)
        side = jnp.where(lane >= LANES - 3, left, jnp.where(lane < 3, right, 0.0))
        first[row, :, 0:col_count] = main
        first[row, :, col_count:] = side

    def smoothed(source, row):
        def weight(i):
            return weights_ref[i, pl.ds(row, 1), :]

        field = source[row]
        value = weight(0) * field + weight(1) * source[row - 1] + weight(2) * source[row + 1]
        value = value + weight(3) * pltpu.roll(field, 1, 1)
        return value + weight(4) * pltpu.roll(field, width - 1, 1)

    @pl.loop(1, tall - 1)
    def _(row):
        second[row] = smoothed(first, row)

    @pl.loop(2, tall - 2)
    def _(row):
        first[row] = smoothed(second, row)

    for row in range(row_count):
        out_ref[:, row, :] = smoothed(first, row + SMOOTH)[:, :col_count]


def border_moves(axes, count_ch):
    rows, cols = axes

    def moves(steps):
        pairs = []
        for row in range(rows):
            for col in range(cols):
                for ch, (down, across) in steps.items():
                    if 0 <= row + down < rows and 0 <= col + across < cols:
                        source = (row * cols + col) * count_ch + ch
                        target = ((row + down) * cols + col + across) * count_ch + ch
                        pairs.append((source, target))
        return pairs

    straight = {ch: (1, 0) for ch in range(3)} | {ch: (-1, 0) for ch in range(3, 6)}
    straight |= {6: (0, 1), 7: (0, -1)}
    return moves(straight), moves({6: (1, 1), 7: (1, -1)}), moves({6: (-1, 1), 7: (-1, -1)})


def shards(spectra, pixel_factor, channel_factor, labels):
    rank, row_count, col_count = pixel_factor.shape
    channels = spectra.shape[0]
    shares = lax.axis_size("ch")
    place = lax.axis_index("ch")
    pixels = row_count * col_count
    strip = row_count // shares + 1

    marks = with_borders(labels + 1, (("row", 0), ("col", 1)), SMOOTH).astype(jnp.float32)
    pad = jnp.zeros((marks.shape[0], LANES - 2 * SMOOTH), jnp.float32)
    marks = jnp.concatenate([marks[:, SMOOTH:], pad, marks[:, :SMOOTH]], axis=1)
    marks = jnp.pad(marks, ((0, -marks.shape[0] % 8), (0, 0)))

    f32 = jnp.float32
    operands = (place.reshape(1), spectra, pixel_factor)
    sums, send, own = kernel_call(
        gram_kernel,
        (
            jax.ShapeDtypeStruct(((rank + channels) // 2, 2 * rank), f32),
            jax.ShapeDtypeStruct((shares, strip, channels, col_count), f32),
            jax.ShapeDtypeStruct((strip, rank, col_count), f32),
        ),
        scratch_shapes=[
            pltpu.VMEM((shares, strip, rank, col_count), f32),
            pltpu.VMEM((4 * rank, pixels), jnp.bfloat16),
            pltpu.VMEM((2 * rank, pixels), jnp.bfloat16),
        ],
        smem=1,
        operands=operands,
        flops=16 * rank * rank * pixels,
    )
    data = lax.all_to_all(send, "ch", 0, 0, tiled=True)
    sums = copies_of_all(doubled_sum(sums, "col"), "row")
    new_channel, copies = kernel_call(
        channel_kernel,
        (
            jax.ShapeDtypeStruct((channels, rank), f32),
            jax.ShapeDtypeStruct((shares, channels // 2, 2 * rank), f32),
        ),
        operands=(sums, channel_factor.T),
    )
    copies = lax.all_to_all(copies, "ch", 0, 0, tiled=True)
    raised = kernel_call(
        raise_kernel,
        jax.ShapeDtypeStruct((strip, rank, col_count), f32),
        operands=(copies, data, own),
        flops=8 * rank * (rank + channels * shares) * strip * col_count,
    )
    piece = raised[strip - 1]
    axes = (lax.axis_size("row"), lax.axis_size("col"))
    straight, below, above = border_moves(axes, shares)
    everywhere = ("row", "col", "ch")
    corner = piece[:, :LANES]
    piece = lax.ppermute(piece, everywhere, straight)
    below = lax.ppermute(corner, everywhere, below)
    above = lax.ppermute(corner, everywhere, above)
    lane = lax.broadcasted_iota(jnp.int32, corner.shape, 1)
    corner = jnp.where(lane >= LANES // 2, below, above)
    sides = jnp.concatenate([piece[:, :LANES], corner], axis=1)
    piece = jnp.where(place >= 6, sides, piece)
    gathered = copies_of_all(jnp.concatenate([raised[: strip - 1], piece[None]], axis=0), "ch")
    tall = row_count + 2 * SMOOTH
    width = col_count + LANES
    field = kernel_call(
        smooth_kernel,
        jax.ShapeDtypeStruct((rank, row_count, col_count), f32),
        scratch_shapes=[
            pltpu.VMEM((tall, rank, width), f32),
            pltpu.VMEM((tall, rank, width), f32),
            pltpu.VMEM((5,) + marks.shape, f32),
        ],
        operands=(marks, gathered),
    )
    return (field, new_channel.T)


def solution(mesh):
    placed = (P("ch", "row", "col"), P(None, "row", "col"), P(None, "ch"), P("row", "col"))
    return jax.shard_map(
        shards,
        mesh=mesh,
        in_specs=placed,
        out_specs=(P(None, "row", "col"), P(None, "ch")),
        check_vma=False,
    )
```

```python
import jax
import jax.numpy as jnp
from jax import lax
from jax.experimental import pallas as pl
from jax.experimental.pallas import tpu as pltpu
from jax.sharding import PartitionSpec as P

SMOOTH = 3
LANES = 128
TILE = 8
epsilon = 1e-09
VMEM_LIMIT = 48 * 1024 * 1024


def doubled_sum(value, axis):
    count = lax.axis_size(axis)
    distance = 1
    while distance < count:
        value = value + lax.ppermute(value, axis, [(i, i ^ distance) for i in range(count)])
        distance *= 2
    return value


def copies_of_all(value, axis):
    count = lax.axis_size(axis)
    copies = jnp.broadcast_to(value[None], (count,) + value.shape)
    return lax.all_to_all(copies, axis, 0, 0, tiled=True)


def kernel_call(kernel, out_shape, scratch_shapes=(), smem=0, waits=0, apart=None, aliases={}, operands=(), flops=0):
    traffic = sum(x.size * 4 for x in operands) + sum(x.size * 4 for x in jax.tree.leaves(out_shape))
    in_specs = [
        pl.BlockSpec(memory_space=pltpu.SMEM if i < smem else pltpu.VMEM)
        for i in range(len(operands) - waits)
    ]
    in_specs += [pl.BlockSpec(memory_space=pl.ANY)] * waits
    return pl.pallas_call(
        kernel,
        out_shape=out_shape,
        in_specs=in_specs,
        out_specs=jax.tree.map(
            lambda x: pl.BlockSpec(memory_space=pl.ANY if x.shape == apart else pltpu.VMEM), out_shape
        ),
        scratch_shapes=scratch_shapes,
        input_output_aliases=aliases,
        compiler_params=pltpu.CompilerParams(vmem_limit_bytes=VMEM_LIMIT),
        cost_estimate=pl.CostEstimate(flops=flops, bytes_accessed=traffic, transcendentals=0),
    )(*operands)


def split(value):
    high = value.astype(jnp.bfloat16)
    low = (value - high.astype(jnp.float32)).astype(jnp.bfloat16)
    return high, low


def gram_kernel(
    place_ref, data_ref, factor_ref, labels_ref, sums_ref, send_ref, own_ref, rows_ref, wide, tall
):
    channels, row_count, col_count = data_ref.shape
    rank = factor_ref.shape[0]
    both = rank + channels
    half = 2 * rank
    lane = lax.broadcasted_iota(jnp.int32, (both + TILE, LANES), 1)
    sides = [jnp.zeros((both + TILE, LANES), jnp.float32)] * 2
    blank = jnp.zeros((half - both, col_count), jnp.bfloat16)
    none = jnp.zeros((both + TILE, col_count - LANES), jnp.float32)

    def keep(strip, at, factor, data, marks):
        send_ref[strip, at] = data
        rows_ref[strip, at, :rank] = factor
        rows_ref[strip, at, rank:] = marks

    for row in range(row_count):
        if row % 8 == 0:
            eight_data = jnp.swapaxes(data_ref[:, row : row + 8, :], 0, 1)
            eight_factor = jnp.swapaxes(factor_ref[:, row : row + 8, :], 0, 1)
        data, factor = eight_data[row % 8], eight_factor[row % 8]
        marks = (labels_ref[row : row + 1, :] + 1).astype(jnp.float32)
        marks = jnp.broadcast_to(marks, (TILE, col_count))
        keep(row // 4, row % 4, factor, data, marks)
        if row >= row_count - SMOOTH:
            keep(row - row_count + SMOOTH, 4, factor, data, marks)
        if row < SMOOTH:
            keep(SMOOTH + row, 4, factor, data, marks)
        value = jnp.concatenate([factor, data, marks], axis=0)
        here = (lane >= 3 * row) & (lane < 3 * row + 3)
        last = pltpu.roll(value[:, col_count - LANES :], 3 * row + 3, 1)
        sides[0] = jnp.where(here, last, sides[0])
        sides[1] = jnp.where(here, pltpu.roll(value[:, :LANES], 3 * row, 1), sides[1])
        high, low = split(value[:both])
        columns = slice(row * col_count, (row + 1) * col_count)
        wide[0:both, columns] = high
        wide[both:half, columns] = blank
        wide[half : half + both, columns] = low
        wide[half + both :, columns] = blank
        tall[0:rank, columns] = high[:rank]
        tall[rank:half, columns] = low[:rank]
    for side in range(2):
        value = jnp.concatenate([sides[side], none], axis=1)
        keep(6 + side, 4, value[:rank], value[rank:both], value[both:])
    own_ref[...] = rows_ref[place_ref[0]]
    products = lax.dot_general(
        wide[...], tall[...], (((1,), (1,)), ((), ())), preferred_element_type=jnp.float32
    )
    products = products[0:half] + products[half:]
    products = products + pltpu.roll(products, rank, 1)
    packed = both // 2
    sums_ref[...] = jnp.where(lane[:packed] < rank, products[0:packed], products[packed:both])


def channel_kernel(sums_ref, factor_ref, data_ref, new_ref, copies_ref):
    channels, rank = factor_ref.shape
    total = sums_ref[...]
    total = jnp.concatenate([total, pltpu.roll(total, rank, 1)], axis=0)[:, :rank]
    gram, top = total[:rank], total[rank:]
    factor = factor_ref[...]
    lower = lax.dot_general(
        factor,
        gram,
        (((1,), (1,)), ((), ())),
        precision=lax.Precision.HIGHEST,
        preferred_element_type=jnp.float32,
    )
    new = factor * top / (lower + epsilon)
    new_ref[...] = new
    packed = channels // 2
    new = jnp.concatenate([new[:packed], new[packed:]], axis=1)
    for i in range(copies_ref.shape[0]):
        copies_ref[i] = new


def factors(new_ref, rank):
    parts = []
    for i in range(new_ref.shape[0]):
        parts += [new_ref[i], pltpu.roll(new_ref[i], rank, 1)]
    new = jnp.transpose(jnp.concatenate(parts, axis=0))[:rank]
    gram = lax.dot_general(
        new,
        new,
        (((1,), (1,)), ((), ())),
        precision=lax.Precision.HIGHEST,
        preferred_element_type=jnp.float32,
    )
    return jnp.concatenate(split(new), axis=0), jnp.concatenate(split(gram), axis=0)


def raised_row(new, gram, data_ref, own_ref, row):
    rank = new.shape[0] // 2

    def product(left, right):
        high, low = split(right)
        both = jnp.dot(left, high, preferred_element_type=jnp.float32)
        both = both + jnp.dot(left, low, preferred_element_type=jnp.float32)
        return both[:rank] + both[rank:]

    data = jnp.concatenate([data_ref[i, row] for i in range(data_ref.shape[0])], axis=0)
    factor = own_ref[row, :rank]
    return factor * product(new, data) / (product(gram, factor) + epsilon)


def border_kernel(new_ref, data_ref, own_ref, piece_ref, corner_ref):
    rank = own_ref.shape[1] - TILE
    new, gram = factors(new_ref, rank)
    last = own_ref.shape[0] - 1
    piece_ref[:rank] = raised_row(new, gram, data_ref, own_ref, last)
    piece_ref[rank:] = own_ref[last, rank:]
    corner_ref[...] = piece_ref[:, :LANES]


def raise_kernel(new_ref, data_ref, own_ref, raised_ref):
    new, gram = factors(new_ref, raised_ref.shape[1])
    for row in range(raised_ref.shape[0]):
        raised_ref[row] = raised_row(new, gram, data_ref, own_ref, row)


def join_kernel(place_ref, straight_ref, below_ref, above_ref, raised_ref, parts_ref):
    shares, _, share, _ = parts_ref.shape
    strip = raised_ref.shape[0]
    lane = lax.broadcasted_iota(jnp.int32, below_ref.shape, 1)
    corner = jnp.where(lane >= LANES // 2, below_ref[...], above_ref[...])
    side = place_ref[0] >= shares - 2
    corner = jnp.where(side, corner, straight_ref[:, LANES:])
    rank = shares * share
    for i in range(shares):
        ranks = slice(i * share, (i + 1) * share)
        for row in range(strip):
            parts_ref[i, row] = raised_ref[row, ranks]
        for at, rows in ((strip, ranks), (strip + 1, slice(rank, rank + TILE))):
            parts_ref[i, at, :, :LANES] = straight_ref[rows, :LANES]
            parts_ref[i, at, :, LANES:] = corner[rows]


def side_of(left, right, at):
    lane = lax.broadcasted_iota(jnp.int32, left.shape, 1)
    left = pltpu.roll(left, (LANES - 3 - at) % LANES, 1)
    right = pltpu.roll(right, (LANES - at) % LANES, 1)
    return jnp.where(lane >= LANES - 3, left, jnp.where(lane < 3, right, 0.0))


def smooth_kernel(labels_ref, parts_ref, copies_ref, first, second, marks_ref, weights_ref, done_ref, written):
    share, row_count, col_count = done_ref.shape
    width = first.shape[2]
    strip = parts_ref.shape[1] - 2
    tall = row_count + 2 * SMOOTH
    marks_ref[...] = jnp.zeros(marks_ref.shape, jnp.float32)
    for row in range(tall):
        inner = row - SMOOTH
        if 0 <= inner < row_count:
            main = parts_ref[inner // strip, inner % strip]
            marks = (labels_ref[inner : inner + 1, :] + 1).astype(jnp.float32)
            start, at = 0, 3 * inner
        else:
            piece = row if inner < 0 else SMOOTH + inner - row_count
            main, marks = parts_ref[piece, strip], parts_ref[piece, strip + 1][:1]
            start, at = LANES, 3 * (inner % row_count)
        first[row, :, :col_count] = main
        marks_ref[row : row + 1, :col_count] = marks
        columns = slice(start, start + LANES)
        left, right = parts_ref[6, strip, :, columns], parts_ref[7, strip, :, columns]
        first[row, :, col_count:] = side_of(left, right, at)
        left, right = parts_ref[6, strip + 1, :, columns], parts_ref[7, strip + 1, :, columns]
        marks_ref[row : row + 1, col_count:] = side_of(left, right, at)[:1]
    marks = marks_ref[...]
    total = jnp.ones(marks.shape, jnp.float32)
    found = []
    for shift, axis in ((1, 0), (marks.shape[0] - 1, 0), (1, 1), (width - 1, 1)):
        neighbour = pltpu.roll(marks, shift, axis)
        weight = jnp.where(neighbour == marks, 1.0, 0.25)
        weight = jnp.where(neighbour == 0.0, 0.0, weight)
        found.append(weight)
        total = total + weight
    inverse = 1.0 / total
    weights_ref[0] = inverse
    for i, weight in enumerate(found):
        weights_ref[1 + i] = weight * inverse

    def smoothed(source, row):
        def weight(i):
            return weights_ref[i, row : row + 1, :]

        field = source[row]
        value = weight(0) * field + weight(1) * source[row - 1] + weight(2) * source[row + 1]
        value = value + weight(3) * pltpu.roll(field, 1, 1)
        return value + weight(4) * pltpu.roll(field, width - 1, 1)

    source, target = first, second
    for step in range(1, SMOOTH):
        for row in range(step, tall - step):
            target[row] = smoothed(source, row)
        source, target = target, source
    for top in range(0, row_count, 8):
        rows = [smoothed(source, top + SMOOTH + i)[None, :, :col_count] for i in range(8)]
        done_ref[:, top : top + 8, :] = jnp.swapaxes(jnp.concatenate(rows, axis=0), 0, 1)
    moves = [
        pltpu.make_async_copy(done_ref, copies_ref.at[i], written.at[i])
        for i in range(copies_ref.shape[0])
    ]
    for move in moves:
        move.start()
    for move in moves:
        move.wait()


def border_moves(axes, count_ch):
    rows, cols = axes

    def moves(steps):
        pairs = []
        for row in range(rows):
            for col in range(cols):
                for ch, (down, across) in steps.items():
                    if 0 <= row + down < rows and 0 <= col + across < cols:
                        source = (row * cols + col) * count_ch + ch
                        target = ((row + down) * cols + col + across) * count_ch + ch
                        pairs.append((source, target))
        return pairs

    straight = {ch: (1, 0) for ch in range(3)} | {ch: (-1, 0) for ch in range(3, 6)}
    straight |= {6: (0, 1), 7: (0, -1)}
    return moves(straight), moves({6: (1, 1), 7: (1, -1)}), moves({6: (-1, 1), 7: (-1, -1)})


def shards(spectra, pixel_factor, channel_factor, labels):
    rank, row_count, col_count = pixel_factor.shape
    channels = spectra.shape[0]
    shares = lax.axis_size("ch")
    place = lax.axis_index("ch")
    pixels = row_count * col_count
    strip = row_count // shares + 1

    f32 = jnp.float32
    place = place.reshape(1)
    operands = (place, spectra, pixel_factor, labels)
    sums, send, own = kernel_call(
        gram_kernel,
        (
            jax.ShapeDtypeStruct(((rank + channels) // 2, 2 * rank), f32),
            jax.ShapeDtypeStruct((shares, strip, channels, col_count), f32),
            jax.ShapeDtypeStruct((strip, rank + TILE, col_count), f32),
        ),
        scratch_shapes=[
            pltpu.VMEM((shares, strip, rank + TILE, col_count), f32),
            pltpu.VMEM((4 * rank, pixels), jnp.bfloat16),
            pltpu.VMEM((2 * rank, pixels), jnp.bfloat16),
        ],
        smem=1,
        operands=operands,
        flops=16 * rank * rank * pixels,
    )
    data = lax.all_to_all(send, "ch", 0, 0, tiled=True)
    sums = doubled_sum(doubled_sum(sums, "row"), "col")
    new_channel, copies = kernel_call(
        channel_kernel,
        (
            jax.ShapeDtypeStruct((channels, rank), f32),
            jax.ShapeDtypeStruct((shares, channels // 2, 2 * rank), f32),
        ),
        waits=1,
        operands=(sums, channel_factor.T, data),
    )
    copies = lax.all_to_all(copies, "ch", 0, 0, tiled=True)
    flops = 8 * rank * (rank + channels * shares) * col_count
    piece, corner = kernel_call(
        border_kernel,
        (
            jax.ShapeDtypeStruct((rank + TILE, col_count), f32),
            jax.ShapeDtypeStruct((rank + TILE, LANES), f32),
        ),
        operands=(copies, data, own),
        flops=flops,
    )
    raised = kernel_call(
        raise_kernel,
        jax.ShapeDtypeStruct((strip - 1, rank, col_count), f32),
        operands=(copies, data, own),
        flops=4 * flops,
    )
    axes = (lax.axis_size("row"), lax.axis_size("col"))
    straight, below, above = border_moves(axes, shares)
    everywhere = ("row", "col", "ch")
    straight = lax.ppermute(piece, everywhere, straight)
    below = lax.ppermute(corner, everywhere, below)
    above = lax.ppermute(corner, everywhere, above)
    share = rank // shares
    parts = kernel_call(
        join_kernel,
        jax.ShapeDtypeStruct((shares, strip + 1, share, col_count), f32),
        smem=1,
        operands=(place, straight, below, above, raised),
    )
    parts = lax.all_to_all(parts, "ch", 0, 0, tiled=True)
    tall = row_count + 2 * SMOOTH
    width = col_count + LANES
    field = (shares, share, row_count, col_count)
    field = kernel_call(
        smooth_kernel,
        jax.ShapeDtypeStruct(field, f32),
        scratch_shapes=[
            pltpu.VMEM((tall, share, width), f32),
            pltpu.VMEM((tall, share, width), f32),
            pltpu.VMEM((tall + -tall % TILE, width), f32),
            pltpu.VMEM((5, tall + -tall % TILE, width), f32),
            pltpu.VMEM(field[1:], f32),
            pltpu.SemaphoreType.DMA((shares,)),
        ],
        apart=field,
        operands=(labels, parts),
    )
    field = lax.all_to_all(field, "ch", 0, 0, tiled=True).reshape(rank, row_count, col_count)
    return (field, new_channel.T)


def solution(mesh):
    placed = (P("ch", "row", "col"), P(None, "row", "col"), P(None, "ch"), P("row", "col"))
    return jax.shard_map(
        shards,
        mesh=mesh,
        in_specs=placed,
        out_specs=(P(None, "row", "col"), P(None, "ch")),
        check_vma=False,
    )
```

```python
import jax
import jax.numpy as jnp
from jax import lax
from jax.experimental import pallas as pl
from jax.experimental.pallas import tpu as pltpu
from jax.sharding import PartitionSpec as P

SMOOTH = 3
LANES = 128
TILE = 8
epsilon = 1e-09
VMEM_LIMIT = 48 * 1024 * 1024
FIRST_LIMIT = 62 * 1024 * 1024


def pair_sum(value, axis, distance):
    count = lax.axis_size(axis)
    return value + lax.ppermute(value, axis, [(i, i ^ distance) for i in range(count)])


def four_sum(value, axis, near, far):
    count = lax.axis_size(axis)
    farthest, middle, close = (
        lax.ppermute(value, axis, [(i, i ^ distance) for i in range(count)])
        for distance in (near + far, far, near)
    )
    return (value + close) + (middle + farthest)


def copies_of_all(value, axis):
    count = lax.axis_size(axis)
    copies = jnp.broadcast_to(value[None], (count,) + value.shape)
    return lax.all_to_all(copies, axis, 0, 0, tiled=True)


def kernel_call(
    kernel, out_shape, scratch_shapes=(), smem=0, waits=0, apart=None, operands=(), flops=0, limit=VMEM_LIMIT
):
    traffic = sum(x.size * 4 for x in operands) + sum(x.size * 4 for x in jax.tree.leaves(out_shape))
    in_specs = [
        pl.BlockSpec(memory_space=pltpu.SMEM if i < smem else pltpu.VMEM)
        for i in range(len(operands) - waits)
    ]
    in_specs += [pl.BlockSpec(memory_space=pl.ANY)] * waits
    return pl.pallas_call(
        kernel,
        out_shape=out_shape,
        in_specs=in_specs,
        out_specs=jax.tree.map(
            lambda x: pl.BlockSpec(memory_space=pl.ANY if x.shape == apart else pltpu.VMEM), out_shape
        ),
        scratch_shapes=scratch_shapes,
        compiler_params=pltpu.CompilerParams(vmem_limit_bytes=limit),
        cost_estimate=pl.CostEstimate(flops=flops, bytes_accessed=traffic, transcendentals=0),
    )(*operands)


def split(value):
    high = value.astype(jnp.bfloat16)
    low = (value - high.astype(jnp.float32)).astype(jnp.bfloat16)
    return high, low


def side_pieces(value, row, sides):
    lane = lax.broadcasted_iota(jnp.int32, (value.shape[0], LANES), 1)
    here = (lane >= 3 * row) & (lane < 3 * row + 3)
    last = pltpu.roll(value[:, value.shape[1] - LANES :], 3 * row + 3, 1)
    first = pltpu.roll(value[:, :LANES], 3 * row, 1)
    return jnp.where(here, last, sides[0]), jnp.where(here, first, sides[1])


def strips_kernel(data_ref, send_ref):
    channels, row_count, col_count = data_ref.shape
    sides = (jnp.zeros((channels, LANES), jnp.float32),) * 2
    for row in range(row_count):
        if row % 8 == 0:
            eight = jnp.swapaxes(data_ref[:, row : row + 8, :], 0, 1)
        data = eight[row % 8]
        send_ref[row // 4, row % 4] = data
        if row >= row_count - SMOOTH:
            send_ref[row - row_count + SMOOTH, 4] = data
        if row < SMOOTH:
            send_ref[SMOOTH + row, 4] = data
        sides = side_pieces(data, row, sides)
    for i in range(2):
        send_ref[6 + i, 4, :, :LANES] = sides[i]
        send_ref[6 + i, 4, :, LANES:] = jnp.zeros((channels, col_count - LANES), jnp.float32)


def gram_kernel(place_ref, send_ref, factor_ref, labels_ref, sums_ref, own_ref, rows_ref, wide, tall):
    channels = send_ref.shape[2]
    rank, row_count, col_count = factor_ref.shape
    both = rank + channels
    half = 2 * rank
    for top in (both, half + both):
        wide[top : top + half - both] = jnp.zeros((half - both, wide.shape[1]), jnp.bfloat16)
    sides = (jnp.zeros((rank + TILE, LANES), jnp.float32),) * 2
    for row in range(row_count):
        if row % 8 == 0:
            eight = jnp.swapaxes(factor_ref[:, row : row + 8, :], 0, 1)
        factor = eight[row % 8]
        marks = (labels_ref[row : row + 1, :] + 1).astype(jnp.float32)
        marked = jnp.concatenate([factor, jnp.broadcast_to(marks, (TILE, col_count))], axis=0)
        rows_ref[row // 4, row % 4] = marked
        if row >= row_count - SMOOTH:
            rows_ref[row - row_count + SMOOTH, 4] = marked
        if row < SMOOTH:
            rows_ref[SMOOTH + row, 4] = marked
        sides = side_pieces(marked, row, sides)
        high, low = split(jnp.concatenate([factor, send_ref[row // 4, row % 4]], axis=0))
        columns = slice(row * col_count, (row + 1) * col_count)
        wide[0:both, columns] = high
        wide[half : half + both, columns] = low
        tall[0:rank, columns] = high[:rank]
        tall[rank:half, columns] = low[:rank]
    for i in range(2):
        rows_ref[6 + i, 4, :, :LANES] = sides[i]
        rows_ref[6 + i, 4, :, LANES:] = jnp.zeros((rank + TILE, col_count - LANES), jnp.float32)
    own_ref[...] = rows_ref[place_ref[0]]
    products = lax.dot_general(
        wide[...], tall[...], (((1,), (1,)), ((), ())), preferred_element_type=jnp.float32
    )
    products = products[0:half] + products[half:]
    products = products + pltpu.roll(products, rank, 1)
    packed = both // 2
    lane = lax.broadcasted_iota(jnp.int32, (packed, LANES), 1)
    sums_ref[...] = jnp.where(lane < rank, products[0:packed], products[packed:both])


def channel_kernel(sums_ref, factor_ref, data_ref, new_ref, copies_ref):
    channels, rank = factor_ref.shape
    total = sums_ref[...]
    total = jnp.concatenate([total, pltpu.roll(total, rank, 1)], axis=0)[:, :rank]
    gram, top = total[:rank], total[rank:]
    factor = factor_ref[...]
    lower = lax.dot_general(
        factor,
        gram,
        (((1,), (1,)), ((), ())),
        precision=lax.Precision.HIGHEST,
        preferred_element_type=jnp.float32,
    )
    new = factor * top / (lower + epsilon)
    new_ref[...] = new
    packed = channels // 2
    new = jnp.concatenate([new[:packed], new[packed:]], axis=1)
    for i in range(copies_ref.shape[0]):
        copies_ref[i] = new


def factors(new_ref, rank):
    parts = []
    for i in range(new_ref.shape[0]):
        parts += [new_ref[i], pltpu.roll(new_ref[i], rank, 1)]
    new = jnp.transpose(jnp.concatenate(parts, axis=0))[:rank]
    gram = lax.dot_general(
        new,
        new,
        (((1,), (1,)), ((), ())),
        precision=lax.Precision.HIGHEST,
        preferred_element_type=jnp.float32,
    )
    return jnp.concatenate(split(new), axis=0), jnp.concatenate(split(gram), axis=0)


def raised_row(new, gram, data_ref, own_ref, row):
    rank = new.shape[0] // 2

    def product(left, right):
        high, low = split(right)
        both = jnp.dot(left, high, preferred_element_type=jnp.float32)
        both = both + jnp.dot(left, low, preferred_element_type=jnp.float32)
        return both[:rank] + both[rank:]

    data = jnp.concatenate([data_ref[i, row] for i in range(data_ref.shape[0])], axis=0)
    factor = own_ref[row, :rank]
    return factor * product(new, data) / (product(gram, factor) + epsilon)


def border_kernel(new_ref, data_ref, own_ref, piece_ref, corner_ref):
    rank = own_ref.shape[1] - TILE
    new, gram = factors(new_ref, rank)
    last = own_ref.shape[0] - 1
    piece_ref[:rank] = raised_row(new, gram, data_ref, own_ref, last)
    piece_ref[rank:] = own_ref[last, rank:]
    corner_ref[...] = piece_ref[:, :LANES]


def raise_kernel(new_ref, data_ref, own_ref, raised_ref):
    new, gram = factors(new_ref, raised_ref.shape[1])
    for row in range(raised_ref.shape[0]):
        raised_ref[row] = raised_row(new, gram, data_ref, own_ref, row)


def join_kernel(place_ref, straight_ref, below_ref, above_ref, raised_ref, parts_ref):
    shares, _, share, _ = parts_ref.shape
    strip = raised_ref.shape[0]
    lane = lax.broadcasted_iota(jnp.int32, below_ref.shape, 1)
    corner = jnp.where(lane >= LANES // 2, below_ref[...], above_ref[...])
    side = place_ref[0] >= shares - 2
    corner = jnp.where(side, corner, straight_ref[:, LANES:])
    rank = shares * share
    for i in range(shares):
        ranks = slice(i * share, (i + 1) * share)
        for row in range(strip):
            parts_ref[i, row] = raised_ref[row, ranks]
        for at, rows in ((strip, ranks), (strip + 1, slice(rank, rank + TILE))):
            parts_ref[i, at, :, :LANES] = straight_ref[rows, :LANES]
            parts_ref[i, at, :, LANES:] = corner[rows]


def side_of(left, right, at):
    lane = lax.broadcasted_iota(jnp.int32, left.shape, 1)
    left = pltpu.roll(left, (LANES - 3 - at) % LANES, 1)
    right = pltpu.roll(right, (LANES - at) % LANES, 1)
    return jnp.where(lane >= LANES - 3, left, jnp.where(lane < 3, right, 0.0))


def smooth_kernel(labels_ref, parts_ref, copies_ref, first, second, marks_ref, weights_ref, done_ref, written):
    share, row_count, col_count = done_ref.shape
    width = first.shape[2]
    strip = parts_ref.shape[1] - 2
    tall = row_count + 2 * SMOOTH
    marks_ref[...] = jnp.zeros(marks_ref.shape, jnp.float32)
    for row in range(tall):
        inner = row - SMOOTH
        if 0 <= inner < row_count:
            main = parts_ref[inner // strip, inner % strip]
            marks = (labels_ref[inner : inner + 1, :] + 1).astype(jnp.float32)
            start, at = 0, 3 * inner
        else:
            piece = row if inner < 0 else SMOOTH + inner - row_count
            main, marks = parts_ref[piece, strip], parts_ref[piece, strip + 1][:1]
            start, at = LANES, 3 * (inner % row_count)
        first[row, :, :col_count] = main
        marks_ref[row : row + 1, :col_count] = marks
        columns = slice(start, start + LANES)
        left, right = parts_ref[6, strip, :, columns], parts_ref[7, strip, :, columns]
        first[row, :, col_count:] = side_of(left, right, at)
        left, right = parts_ref[6, strip + 1, :, columns], parts_ref[7, strip + 1, :, columns]
        marks_ref[row : row + 1, col_count:] = side_of(left, right, at)[:1]
    marks = marks_ref[...]
    total = jnp.ones(marks.shape, jnp.float32)
    found = []
    for shift, axis in ((1, 0), (marks.shape[0] - 1, 0), (1, 1), (width - 1, 1)):
        neighbour = pltpu.roll(marks, shift, axis)
        weight = jnp.where(neighbour == marks, 1.0, 0.25)
        weight = jnp.where(neighbour == 0.0, 0.0, weight)
        found.append(weight)
        total = total + weight
    inverse = 1.0 / total
    weights_ref[0] = inverse
    for i, weight in enumerate(found):
        weights_ref[1 + i] = weight * inverse

    def smoothed(source, row):
        def weight(i):
            return weights_ref[i, row : row + 1, :]

        field = source[row]
        value = weight(0) * field + weight(1) * source[row - 1] + weight(2) * source[row + 1]
        value = value + weight(3) * pltpu.roll(field, 1, 1)
        return value + weight(4) * pltpu.roll(field, width - 1, 1)

    source, target = first, second
    for step in range(1, SMOOTH):
        for row in range(step, tall - step):
            target[row] = smoothed(source, row)
        source, target = target, source
    for top in range(0, row_count, 8):
        rows = [smoothed(source, top + SMOOTH + i)[None, :, :col_count] for i in range(8)]
        done_ref[:, top : top + 8, :] = jnp.swapaxes(jnp.concatenate(rows, axis=0), 0, 1)
    moves = [
        pltpu.make_async_copy(done_ref, copies_ref.at[pl.ds(i * share, share)], written.at[i])
        for i in range(parts_ref.shape[0])
    ]
    for move in moves:
        move.start()
    for move in moves:
        move.wait()


def border_moves(axes, count_ch):
    rows, cols = axes

    def moves(steps):
        pairs = []
        for row in range(rows):
            for col in range(cols):
                for ch, (down, across) in steps.items():
                    if 0 <= row + down < rows and 0 <= col + across < cols:
                        source = (row * cols + col) * count_ch + ch
                        target = ((row + down) * cols + col + across) * count_ch + ch
                        pairs.append((source, target))
        return pairs

    straight = {ch: (1, 0) for ch in range(3)} | {ch: (-1, 0) for ch in range(3, 6)}
    straight |= {6: (0, 1), 7: (0, -1)}
    return moves(straight), moves({6: (1, 1), 7: (1, -1)}), moves({6: (-1, 1), 7: (-1, -1)})


def shards(spectra, pixel_factor, channel_factor, labels):
    rank, row_count, col_count = pixel_factor.shape
    channels = spectra.shape[0]
    shares = lax.axis_size("ch")
    place = lax.axis_index("ch")
    pixels = row_count * col_count
    strip = row_count // shares + 1

    f32 = jnp.float32
    place = place.reshape(1)
    send = kernel_call(
        strips_kernel,
        jax.ShapeDtypeStruct((shares, strip, channels, col_count), f32),
        operands=(spectra,),
        limit=FIRST_LIMIT,
    )
    sums, own = kernel_call(
        gram_kernel,
        (
            jax.ShapeDtypeStruct(((rank + channels) // 2, 2 * rank), f32),
            jax.ShapeDtypeStruct((strip, rank + TILE, col_count), f32),
        ),
        scratch_shapes=[
            pltpu.VMEM((shares, strip, rank + TILE, col_count), f32),
            pltpu.VMEM((4 * rank, pixels), jnp.bfloat16),
            pltpu.VMEM((2 * rank, pixels), jnp.bfloat16),
        ],
        smem=1,
        operands=(place, send, pixel_factor, labels),
        flops=16 * rank * rank * pixels,
        limit=FIRST_LIMIT,
    )
    data = lax.all_to_all(send, "ch", 0, 0, tiled=True)
    sums = four_sum(pair_sum(sums, "row", 1), "row", 2, 4)
    sums = pair_sum(pair_sum(sums, "col", 1), "col", 2)
    new_channel, copies = kernel_call(
        channel_kernel,
        (
            jax.ShapeDtypeStruct((channels, rank), f32),
            jax.ShapeDtypeStruct((shares, channels // 2, 2 * rank), f32),
        ),
        waits=1,
        operands=(sums, channel_factor.T, data),
    )
    copies = lax.all_to_all(copies, "ch", 0, 0, tiled=True)
    flops = 8 * rank * (rank + channels * shares) * col_count
    piece, corner = kernel_call(
        border_kernel,
        (
            jax.ShapeDtypeStruct((rank + TILE, col_count), f32),
            jax.ShapeDtypeStruct((rank + TILE, LANES), f32),
        ),
        operands=(copies, data, own),
        flops=flops,
    )
    raised = kernel_call(
        raise_kernel,
        jax.ShapeDtypeStruct((strip - 1, rank, col_count), f32),
        operands=(copies, data, own),
        flops=4 * flops,
    )
    axes = (lax.axis_size("row"), lax.axis_size("col"))
    straight, below, above = border_moves(axes, shares)
    everywhere = ("row", "col", "ch")
    straight = lax.ppermute(piece, everywhere, straight)
    below = lax.ppermute(corner, everywhere, below)
    above = lax.ppermute(corner, everywhere, above)
    share = rank // shares
    parts = kernel_call(
        join_kernel,
        jax.ShapeDtypeStruct((shares, strip + 1, share, col_count), f32),
        smem=1,
        operands=(place, straight, below, above, raised),
    )
    parts = lax.all_to_all(parts, "ch", 0, 0, tiled=True)
    tall = row_count + 2 * SMOOTH
    width = col_count + LANES
    field = (rank, row_count, col_count)
    field = kernel_call(
        smooth_kernel,
        jax.ShapeDtypeStruct(field, f32),
        scratch_shapes=[
            pltpu.VMEM((tall, share, width), f32),
            pltpu.VMEM((tall, share, width), f32),
            pltpu.VMEM((tall + -tall % TILE, width), f32),
            pltpu.VMEM((5, tall + -tall % TILE, width), f32),
            pltpu.VMEM((share, row_count, col_count), f32),
            pltpu.SemaphoreType.DMA((shares,)),
        ],
        apart=field,
        operands=(labels, parts),
    )
    field = lax.all_to_all(field, "ch", 0, 0, tiled=True)
    return (field, new_channel.T)


def solution(mesh):
    placed = (P("ch", "row", "col"), P(None, "row", "col"), P(None, "ch"), P("row", "col"))
    return jax.shard_map(
        shards,
        mesh=mesh,
        in_specs=placed,
        out_specs=(P(None, "row", "col"), P(None, "ch")),
        check_vma=False,
    )
```

```python
import jax
import jax.numpy as jnp
from jax import lax
from jax.experimental import pallas as pl
from jax.experimental.pallas import tpu as pltpu
from jax.sharding import PartitionSpec as P

SMOOTH = 3
LANES = 128
TILE = 8
UPPER = (0, 1, 2)
LOWER = (3, 4, 7)
FIRST, LAST = 5, 6
epsilon = 1e-09
VMEM_LIMIT = 48 * 1024 * 1024
FIRST_LIMIT = 62 * 1024 * 1024


def pair_sum(value, axis, distance):
    count = lax.axis_size(axis)
    return value + lax.ppermute(value, axis, [(i, i ^ distance) for i in range(count)])


def four_sum(value, axis, near, far):
    count = lax.axis_size(axis)
    farthest, middle, close = (
        lax.ppermute(value, axis, [(i, i ^ distance) for i in range(count)])
        for distance in (near + far, far, near)
    )
    return (value + close) + (middle + farthest)


def copies_of_all(value, axis):
    count = lax.axis_size(axis)
    copies = jnp.broadcast_to(value[None], (count,) + value.shape)
    return lax.all_to_all(copies, axis, 0, 0, tiled=True)


def kernel_call(
    kernel, out_shape, scratch_shapes=(), smem=0, waits=0, apart=None, operands=(), flops=0, limit=VMEM_LIMIT
):
    traffic = sum(x.size * 4 for x in operands) + sum(x.size * 4 for x in jax.tree.leaves(out_shape))
    in_specs = [
        pl.BlockSpec(memory_space=pltpu.SMEM if i < smem else pltpu.VMEM)
        for i in range(len(operands) - waits)
    ]
    in_specs += [pl.BlockSpec(memory_space=pl.ANY)] * waits
    return pl.pallas_call(
        kernel,
        out_shape=out_shape,
        in_specs=in_specs,
        out_specs=jax.tree.map(
            lambda x: pl.BlockSpec(memory_space=pl.ANY if x.shape == apart else pltpu.VMEM), out_shape
        ),
        scratch_shapes=scratch_shapes,
        compiler_params=pltpu.CompilerParams(vmem_limit_bytes=limit),
        cost_estimate=pl.CostEstimate(flops=flops, bytes_accessed=traffic, transcendentals=0),
    )(*operands)


def split(value):
    high = value.astype(jnp.bfloat16)
    low = (value - high.astype(jnp.float32)).astype(jnp.bfloat16)
    return high, low


def side_pieces(value, row, sides):
    lane = lax.broadcasted_iota(jnp.int32, (value.shape[0], LANES), 1)
    here = (lane >= 3 * row) & (lane < 3 * row + 3)
    last = pltpu.roll(value[:, value.shape[1] - LANES :], 3 * row + 3, 1)
    first = pltpu.roll(value[:, :LANES], 3 * row, 1)
    return jnp.where(here, last, sides[0]), jnp.where(here, first, sides[1])


def strips_kernel(data_ref, send_ref, taken, held, arrived, written):
    channels, row_count, col_count = data_ref.shape
    groups = row_count // 8
    reads = [
        pltpu.make_async_copy(data_ref.at[:, pl.ds(8 * i, 8)], taken.at[i], arrived.at[i])
        for i in range(groups)
    ]
    writes = [
        pltpu.make_async_copy(
            held.at[pl.ds(2 * i, 2), pl.ds(0, 4)], send_ref.at[pl.ds(2 * i, 2), pl.ds(0, 4)], written.at[i]
        )
        for i in range(groups)
    ]
    writes.append(
        pltpu.make_async_copy(
            held.at[:, pl.ds(4, 1)], send_ref.at[:, pl.ds(4, 1)], written.at[groups]
        )
    )
    for read in reads:
        read.start()
    sides = (jnp.zeros((channels, LANES), jnp.float32),) * 2
    for row in range(row_count):
        if row % 8 == 0:
            reads[row // 8].wait()
            eight = jnp.swapaxes(taken[row // 8], 0, 1)
        data = eight[row % 8]
        held[row // 4, row % 4] = data
        if row >= row_count - SMOOTH:
            held[UPPER[row - row_count + SMOOTH], 4] = data
        if row < SMOOTH:
            held[LOWER[row], 4] = data
        sides = side_pieces(data, row, sides)
        if row % 8 == 7:
            writes[row // 8].start()
    for i, place in enumerate((LAST, FIRST)):
        held[place, 4, :, :LANES] = sides[i]
        held[place, 4, :, LANES:] = jnp.zeros((channels, col_count - LANES), jnp.float32)
    writes[groups].start()
    for write in writes:
        write.wait()


def gram_kernel(data_ref, factor_ref, sums_ref, wide, tall):
    channels = data_ref.shape[0]
    rank, row_count, col_count = factor_ref.shape
    both = rank + channels
    half = 2 * rank
    for top in (both, half + both):
        wide[top : top + half - both] = jnp.zeros((half - both, wide.shape[1]), jnp.bfloat16)
    for row in range(row_count):
        if row % 8 == 0:
            data = jnp.swapaxes(data_ref[:, row : row + 8, :], 0, 1)
            factor = jnp.swapaxes(factor_ref[:, row : row + 8, :], 0, 1)
        high, low = split(jnp.concatenate([factor[row % 8], data[row % 8]], axis=0))
        columns = slice(row * col_count, (row + 1) * col_count)
        wide[0:both, columns] = high
        wide[half : half + both, columns] = low
        tall[0:rank, columns] = high[:rank]
        tall[rank:half, columns] = low[:rank]
    products = lax.dot_general(
        wide[...], tall[...], (((1,), (1,)), ((), ())), preferred_element_type=jnp.float32
    )
    products = products[0:half] + products[half:]
    products = products + pltpu.roll(products, rank, 1)
    packed = both // 2
    lane = lax.broadcasted_iota(jnp.int32, (packed, LANES), 1)
    sums_ref[...] = jnp.where(lane < rank, products[0:packed], products[packed:both])


def own_kernel(place_ref, factor_ref, labels_ref, own_ref, rows_ref):
    rank, row_count, col_count = factor_ref.shape
    sides = (jnp.zeros((rank + TILE, LANES), jnp.float32),) * 2
    for row in range(row_count):
        if row % 8 == 0:
            eight = jnp.swapaxes(factor_ref[:, row : row + 8, :], 0, 1)
        marks = (labels_ref[row : row + 1, :] + 1).astype(jnp.float32)
        marks = jnp.broadcast_to(marks, (TILE, col_count))
        marked = jnp.concatenate([eight[row % 8], marks], axis=0)
        rows_ref[row // 4, row % 4] = marked
        if row >= row_count - SMOOTH:
            rows_ref[UPPER[row - row_count + SMOOTH], 4] = marked
        if row < SMOOTH:
            rows_ref[LOWER[row], 4] = marked
        sides = side_pieces(marked, row, sides)
    for i, place in enumerate((LAST, FIRST)):
        rows_ref[place, 4, :, :LANES] = sides[i]
        rows_ref[place, 4, :, LANES:] = jnp.zeros((rank + TILE, col_count - LANES), jnp.float32)
    own_ref[...] = rows_ref[place_ref[0]]


def channel_kernel(sums_ref, factor_ref, data_ref, own_ref, new_ref, copies_ref):
    channels, rank = factor_ref.shape
    total = sums_ref[...]
    total = jnp.concatenate([total, pltpu.roll(total, rank, 1)], axis=0)[:, :rank]
    gram, top = total[:rank], total[rank:]
    factor = factor_ref[...]
    lower = lax.dot_general(
        factor,
        gram,
        (((1,), (1,)), ((), ())),
        precision=lax.Precision.HIGHEST,
        preferred_element_type=jnp.float32,
    )
    new = factor * top / (lower + epsilon)
    new_ref[...] = new
    packed = channels // 2
    new = jnp.concatenate([new[:packed], new[packed:]], axis=1)
    for i in range(copies_ref.shape[0]):
        copies_ref[i] = new


def factors(new_ref, rank):
    parts = []
    for i in range(new_ref.shape[0]):
        parts += [new_ref[i], pltpu.roll(new_ref[i], rank, 1)]
    new = jnp.transpose(jnp.concatenate(parts, axis=0))[:rank]
    gram = lax.dot_general(
        new,
        new,
        (((1,), (1,)), ((), ())),
        precision=lax.Precision.HIGHEST,
        preferred_element_type=jnp.float32,
    )
    return jnp.concatenate(split(new), axis=0), jnp.concatenate(split(gram), axis=0)


def raised_part(new, gram, data_ref, own_ref, row, columns):
    rank = new.shape[0] // 2

    def product(left, right):
        high, low = split(right)
        both = jnp.dot(left, high, preferred_element_type=jnp.float32)
        both = both + jnp.dot(left, low, preferred_element_type=jnp.float32)
        return both[:rank] + both[rank:]

    shares = data_ref.shape[0]
    data = jnp.concatenate([data_ref[i, row, :, columns] for i in range(shares)], axis=0)
    own = own_ref[row, :, columns]
    factor = own[:rank]
    raised = factor * product(new, data) / (product(gram, factor) + epsilon)
    return jnp.concatenate([raised, own[rank:]], axis=0)


def border_kernel(place_ref, new_ref, data_ref, own_ref, piece_ref, corner_ref):
    height, col_count = piece_ref.shape
    row_count = data_ref.shape[0] * (own_ref.shape[0] - 1)
    new, gram = factors(new_ref, height - TILE)
    piece_ref[...] = raised_part(new, gram, data_ref, own_ref, own_ref.shape[0] - 1, slice(None))
    place = place_ref[0]
    lowest = (place == data_ref.shape[0] - 1).astype(jnp.int32)
    tile = pl.ds(pl.multiple_of(lowest * (col_count - LANES), LANES), LANES)
    lane = lax.broadcasted_iota(jnp.int32, corner_ref.shape, 1)
    corner = jnp.zeros(corner_ref.shape, jnp.float32)
    for i in range(SMOOTH):
        value = raised_part(new, gram, data_ref, own_ref, i + lowest, tile)
        at = 3 * (i + lowest * (row_count - SMOOTH))
        shift = lax.rem(at + 3 * lowest + 2 * LANES, LANES)
        corner = jnp.where((lane >= at) & (lane < at + 3), pltpu.roll(value, shift, 1), corner)
    side = (place == FIRST) | (place == LAST)
    corner_ref[...] = jnp.where(side, piece_ref[:, :LANES], corner)


def raise_kernel(new_ref, data_ref, own_ref, raised_ref):
    rank = raised_ref.shape[1]
    new, gram = factors(new_ref, rank)
    for row in range(raised_ref.shape[0]):
        raised_ref[row] = raised_part(new, gram, data_ref, own_ref, row, slice(None))[:rank]


def join_kernel(straight_ref, corner_ref, raised_ref, parts_ref):
    shares, _, share, _ = parts_ref.shape
    strip = raised_ref.shape[0]
    marks = slice(shares * share, shares * share + TILE)
    for i in range(shares):
        ranks = slice(i * share, (i + 1) * share)
        for row in range(strip):
            parts_ref[i, row] = raised_ref[row, ranks]
        parts_ref[i, strip] = straight_ref[ranks]
        parts_ref[i, strip + 1] = straight_ref[marks]
        parts_ref[i, strip + 2, :, :LANES] = corner_ref[ranks]
        parts_ref[i, strip + 2, :, LANES:] = corner_ref[marks]


def side_of(left, right, at):
    lane = lax.broadcasted_iota(jnp.int32, left.shape, 1)
    left = pltpu.roll(left, (LANES - 3 - at) % LANES, 1)
    right = pltpu.roll(right, (LANES - at) % LANES, 1)
    return jnp.where(lane >= LANES - 3, left, jnp.where(lane < 3, right, 0.0))


def smooth_kernel(labels_ref, parts_ref, copies_ref, first, second, marks_ref, weights_ref, done_ref, written):
    share, row_count, col_count = done_ref.shape
    width = first.shape[2]
    strip = parts_ref.shape[1] - 3
    tall = row_count + 2 * SMOOTH
    marks_ref[...] = jnp.zeros(marks_ref.shape, jnp.float32)

    def tiles(place, row):
        if row == strip:
            return parts_ref[place, row, :, :LANES], parts_ref[place, row + 1, :, :LANES]
        return parts_ref[place, row, :, :LANES], parts_ref[place, row, :, LANES:]

    for row in range(tall):
        inner = row - SMOOTH
        if 0 <= inner < row_count:
            main = parts_ref[inner // strip, inner % strip]
            marks = (labels_ref[inner : inner + 1, :] + 1).astype(jnp.float32)
            left, right = tiles(LAST, strip), tiles(FIRST, strip)
        else:
            piece = UPPER[row] if inner < 0 else LOWER[inner - row_count]
            main, marks = parts_ref[piece, strip], parts_ref[piece, strip + 1][:1]
            places = (parts_ref.shape[0] - 1, FIRST) if inner < 0 else (LAST, 0)
            left, right = (tiles(place, strip + 2) for place in places)
        at = 3 * (inner % row_count)
        first[row, :, :col_count] = main
        first[row, :, col_count:] = side_of(left[0], right[0], at)
        marks_ref[row : row + 1, :col_count] = marks
        marks_ref[row : row + 1, col_count:] = side_of(left[1], right[1], at)[:1]
    marks = marks_ref[...]
    total = jnp.ones(marks.shape, jnp.float32)
    found = []
    for shift, axis in ((1, 0), (marks.shape[0] - 1, 0), (1, 1), (width - 1, 1)):
        neighbour = pltpu.roll(marks, shift, axis)
        weight = jnp.where(neighbour == marks, 1.0, 0.25)
        weight = jnp.where(neighbour == 0.0, 0.0, weight)
        found.append(weight)
        total = total + weight
    inverse = 1.0 / total
    weights_ref[0] = inverse
    for i, weight in enumerate(found):
        weights_ref[1 + i] = weight * inverse

    def smoothed(source, row):
        def weight(i):
            return weights_ref[i, row : row + 1, :]

        field = source[row]
        value = weight(0) * field + weight(1) * source[row - 1] + weight(2) * source[row + 1]
        value = value + weight(3) * pltpu.roll(field, 1, 1)
        return value + weight(4) * pltpu.roll(field, width - 1, 1)

    source, target = first, second
    for step in range(1, SMOOTH):
        for row in range(step, tall - step):
            target[row] = smoothed(source, row)
        source, target = target, source
    for top in range(0, row_count, 8):
        rows = [smoothed(source, top + SMOOTH + i)[None, :, :col_count] for i in range(8)]
        done_ref[:, top : top + 8, :] = jnp.swapaxes(jnp.concatenate(rows, axis=0), 0, 1)
    moves = [
        pltpu.make_async_copy(done_ref, copies_ref.at[pl.ds(i * share, share)], written.at[i])
        for i in range(parts_ref.shape[0])
    ]
    for move in moves:
        move.start()
    for move in moves:
        move.wait()


def border_moves(axes, count_ch):
    rows, cols = axes

    def moves(steps):
        pairs = []
        for row in range(rows):
            for col in range(cols):
                for ch, (down, across) in steps.items():
                    if 0 <= row + down < rows and 0 <= col + across < cols:
                        source = (row * cols + col) * count_ch + ch
                        target = ((row + down) * cols + col + across) * count_ch + ch
                        pairs.append((source, target))
        return pairs

    straight = dict.fromkeys(UPPER, (1, 0)) | dict.fromkeys(LOWER, (-1, 0))
    straight |= {LAST: (0, 1), FIRST: (0, -1)}
    corners = {count_ch - 1: (1, 1), FIRST: (1, -1), LAST: (-1, 1), 0: (-1, -1)}
    return moves(straight), moves(corners)


def shards(spectra, pixel_factor, channel_factor, labels):
    rank, row_count, col_count = pixel_factor.shape
    channels = spectra.shape[0]
    shares = lax.axis_size("ch")
    place = lax.axis_index("ch")
    pixels = row_count * col_count
    strip = row_count // shares + 1

    f32 = jnp.float32
    place = place.reshape(1)
    send = (shares, strip, channels, col_count)
    send = kernel_call(
        strips_kernel,
        jax.ShapeDtypeStruct(send, f32),
        scratch_shapes=[
            pltpu.VMEM((row_count // 8, channels, 8, col_count), f32),
            pltpu.VMEM(send, f32),
            pltpu.SemaphoreType.DMA((row_count // 8,)),
            pltpu.SemaphoreType.DMA((row_count // 8 + 1,)),
        ],
        waits=1,
        apart=send,
        operands=(spectra,),
        limit=FIRST_LIMIT,
    )
    sums = kernel_call(
        gram_kernel,
        jax.ShapeDtypeStruct(((rank + channels) // 2, 2 * rank), f32),
        scratch_shapes=[
            pltpu.VMEM((4 * rank, pixels), jnp.bfloat16),
            pltpu.VMEM((2 * rank, pixels), jnp.bfloat16),
        ],
        operands=(spectra, pixel_factor),
        flops=16 * rank * rank * pixels,
    )
    own = kernel_call(
        own_kernel,
        jax.ShapeDtypeStruct((strip, rank + TILE, col_count), f32),
        scratch_shapes=[pltpu.VMEM((shares, strip, rank + TILE, col_count), f32)],
        smem=1,
        operands=(place, pixel_factor, labels),
    )
    data = lax.all_to_all(send, "ch", 0, 0, tiled=True)
    sums = four_sum(pair_sum(sums, "row", 1), "row", 2, 4)
    sums = pair_sum(pair_sum(sums, "col", 1), "col", 2)
    new_channel, copies = kernel_call(
        channel_kernel,
        (
            jax.ShapeDtypeStruct((channels, rank), f32),
            jax.ShapeDtypeStruct((shares, channels // 2, 2 * rank), f32),
        ),
        waits=2,
        operands=(sums, channel_factor.T, data, own),
    )
    copies = lax.all_to_all(copies, "ch", 0, 0, tiled=True)
    flops = 8 * rank * (rank + channels * shares) * col_count
    piece, corner = kernel_call(
        border_kernel,
        (
            jax.ShapeDtypeStruct((rank + TILE, col_count), f32),
            jax.ShapeDtypeStruct((rank + TILE, LANES), f32),
        ),
        smem=1,
        operands=(place, copies, data, own),
        flops=flops,
    )
    raised = kernel_call(
        raise_kernel,
        jax.ShapeDtypeStruct((strip - 1, rank, col_count), f32),
        operands=(copies, data, own),
        flops=4 * flops,
    )
    axes = (lax.axis_size("row"), lax.axis_size("col"))
    straight, corners = border_moves(axes, shares)
    everywhere = ("row", "col", "ch")
    straight = lax.ppermute(piece, everywhere, straight)
    corner = lax.ppermute(corner, everywhere, corners)
    share = rank // shares
    parts = kernel_call(
        join_kernel,
        jax.ShapeDtypeStruct((shares, strip + 2, share, col_count), f32),
        operands=(straight, corner, raised),
    )
    parts = lax.all_to_all(parts, "ch", 0, 0, tiled=True)
    tall = row_count + 2 * SMOOTH
    width = col_count + LANES
    field = (rank, row_count, col_count)
    field = kernel_call(
        smooth_kernel,
        jax.ShapeDtypeStruct(field, f32),
        scratch_shapes=[
            pltpu.VMEM((tall, share, width), f32),
            pltpu.VMEM((tall, share, width), f32),
            pltpu.VMEM((tall + -tall % TILE, width), f32),
            pltpu.VMEM((5, tall + -tall % TILE, width), f32),
            pltpu.VMEM((share, row_count, col_count), f32),
            pltpu.SemaphoreType.DMA((shares,)),
        ],
        apart=field,
        operands=(labels, parts),
    )
    field = lax.all_to_all(field, "ch", 0, 0, tiled=True)
    return (field, new_channel.T)


def solution(mesh):
    placed = (P("ch", "row", "col"), P(None, "row", "col"), P(None, "ch"), P("row", "col"))
    return jax.shard_map(
        shards,
        mesh=mesh,
        in_specs=placed,
        out_specs=(P(None, "row", "col"), P(None, "ch")),
        check_vma=False,
    )
```

```python
import jax
import jax.numpy as jnp
from jax import lax
from jax.experimental import pallas as pl
from jax.experimental.pallas import tpu as pltpu
from jax.sharding import PartitionSpec as P

SMOOTH = 3
LANES = 128
TILE = 8
UPPER = (0, 1, 2)
LOWER = (3, 4, 7)
FIRST, LAST = 5, 6
epsilon = 1e-09
VMEM_LIMIT = 48 * 1024 * 1024
FIRST_LIMIT = 62 * 1024 * 1024


def pair_sum(value, axis, distance):
    count = lax.axis_size(axis)
    return value + lax.ppermute(value, axis, [(i, i ^ distance) for i in range(count)])


def four_sum(value, axis, near, far):
    count = lax.axis_size(axis)
    farthest, middle, close = (
        lax.ppermute(value, axis, [(i, i ^ distance) for i in range(count)])
        for distance in (near + far, far, near)
    )
    return (value + close) + (middle + farthest)


def copies_of_all(value, axis):
    count = lax.axis_size(axis)
    copies = jnp.broadcast_to(value[None], (count,) + value.shape)
    return lax.all_to_all(copies, axis, 0, 0, tiled=True)


def kernel_call(
    kernel, out_shape, scratch_shapes=(), smem=0, waits=0, apart=None, operands=(), flops=0, limit=VMEM_LIMIT
):
    traffic = sum(x.size * 4 for x in operands) + sum(x.size * 4 for x in jax.tree.leaves(out_shape))
    in_specs = [
        pl.BlockSpec(memory_space=pltpu.SMEM if i < smem else pltpu.VMEM)
        for i in range(len(operands) - waits)
    ]
    in_specs += [pl.BlockSpec(memory_space=pl.ANY)] * waits
    return pl.pallas_call(
        kernel,
        out_shape=out_shape,
        in_specs=in_specs,
        out_specs=jax.tree.map(
            lambda x: pl.BlockSpec(memory_space=pl.ANY if x.shape == apart else pltpu.VMEM), out_shape
        ),
        scratch_shapes=scratch_shapes,
        compiler_params=pltpu.CompilerParams(vmem_limit_bytes=limit),
        cost_estimate=pl.CostEstimate(flops=flops, bytes_accessed=traffic, transcendentals=0),
    )(*operands)


def split(value):
    high = value.astype(jnp.bfloat16)
    low = (value - high.astype(jnp.float32)).astype(jnp.bfloat16)
    return high, low


def side_pieces(value, row, sides):
    lane = lax.broadcasted_iota(jnp.int32, (value.shape[0], LANES), 1)
    here = (lane >= 3 * row) & (lane < 3 * row + 3)
    last = pltpu.roll(value[:, value.shape[1] - LANES :], 3 * row + 3, 1)
    first = pltpu.roll(value[:, :LANES], 3 * row, 1)
    return jnp.where(here, last, sides[0]), jnp.where(here, first, sides[1])


def strips_kernel(data_ref, send_ref, taken, held, arrived, written):
    channels, row_count, col_count = data_ref.shape
    groups = row_count // 8
    reads = [
        pltpu.make_async_copy(data_ref.at[:, pl.ds(8 * i, 8)], taken.at[i], arrived.at[i])
        for i in range(groups)
    ]
    writes = [
        pltpu.make_async_copy(
            held.at[pl.ds(2 * i, 2), pl.ds(0, 4)], send_ref.at[pl.ds(2 * i, 2), pl.ds(0, 4)], written.at[i]
        )
        for i in range(groups)
    ]
    writes.append(
        pltpu.make_async_copy(
            held.at[:, pl.ds(4, 1)], send_ref.at[:, pl.ds(4, 1)], written.at[groups]
        )
    )
    for read in reads:
        read.start()
    sides = (jnp.zeros((channels, LANES), jnp.float32),) * 2
    for row in range(row_count):
        if row % 8 == 0:
            reads[row // 8].wait()
            eight = jnp.swapaxes(taken[row // 8], 0, 1)
        data = eight[row % 8]
        held[row // 4, row % 4] = data
        if row >= row_count - SMOOTH:
            held[UPPER[row - row_count + SMOOTH], 4] = data
        if row < SMOOTH:
            held[LOWER[row], 4] = data
        sides = side_pieces(data, row, sides)
        if row % 8 == 7:
            writes[row // 8].start()
    for i, place in enumerate((LAST, FIRST)):
        held[place, 4, :, :LANES] = sides[i]
        held[place, 4, :, LANES:] = jnp.zeros((channels, col_count - LANES), jnp.float32)
    writes[groups].start()
    for write in writes:
        write.wait()


def gram_kernel(data_ref, factor_ref, sums_ref, wide, tall):
    channels = data_ref.shape[0]
    rank, row_count, col_count = factor_ref.shape
    both = rank + channels
    half = 2 * rank
    for top in (both, half + both):
        wide[top : top + half - both] = jnp.zeros((half - both, wide.shape[1]), jnp.bfloat16)
    for row in range(row_count):
        if row % 8 == 0:
            data = jnp.swapaxes(data_ref[:, row : row + 8, :], 0, 1)
            factor = jnp.swapaxes(factor_ref[:, row : row + 8, :], 0, 1)
        high, low = split(jnp.concatenate([factor[row % 8], data[row % 8]], axis=0))
        columns = slice(row * col_count, (row + 1) * col_count)
        wide[0:both, columns] = high
        wide[half : half + both, columns] = low
        tall[0:rank, columns] = high[:rank]
        tall[rank:half, columns] = low[:rank]
    products = lax.dot_general(
        wide[...], tall[...], (((1,), (1,)), ((), ())), preferred_element_type=jnp.float32
    )
    products = products[0:half] + products[half:]
    products = products + pltpu.roll(products, rank, 1)
    packed = both // 2
    lane = lax.broadcasted_iota(jnp.int32, (packed, LANES), 1)
    sums_ref[...] = jnp.where(lane < rank, products[0:packed], products[packed:both])


def own_kernel(place_ref, factor_ref, labels_ref, own_ref, rows_ref):
    rank, row_count, col_count = factor_ref.shape
    sides = (jnp.zeros((rank + TILE, LANES), jnp.float32),) * 2
    for row in range(row_count):
        if row % 8 == 0:
            eight = jnp.swapaxes(factor_ref[:, row : row + 8, :], 0, 1)
        marks = (labels_ref[row : row + 1, :] + 1).astype(jnp.float32)
        marks = jnp.broadcast_to(marks, (TILE, col_count))
        marked = jnp.concatenate([eight[row % 8], marks], axis=0)
        rows_ref[row // 4, row % 4] = marked
        if row >= row_count - SMOOTH:
            rows_ref[UPPER[row - row_count + SMOOTH], 4] = marked
        if row < SMOOTH:
            rows_ref[LOWER[row], 4] = marked
        sides = side_pieces(marked, row, sides)
    for i, place in enumerate((LAST, FIRST)):
        rows_ref[place, 4, :, :LANES] = sides[i]
        rows_ref[place, 4, :, LANES:] = jnp.zeros((rank + TILE, col_count - LANES), jnp.float32)
    own_ref[...] = rows_ref[place_ref[0]]


def channel_kernel(sums_ref, factor_ref, data_ref, own_ref, new_ref, copies_ref):
    channels, rank = factor_ref.shape
    total = sums_ref[...]
    total = jnp.concatenate([total, pltpu.roll(total, rank, 1)], axis=0)[:, :rank]
    gram, top = total[:rank], total[rank:]
    factor = factor_ref[...]
    lower = lax.dot_general(
        factor,
        gram,
        (((1,), (1,)), ((), ())),
        precision=lax.Precision.HIGHEST,
        preferred_element_type=jnp.float32,
    )
    new = factor * top / (lower + epsilon)
    new_ref[...] = new
    packed = channels // 2
    new = jnp.concatenate([new[:packed], new[packed:]], axis=1)
    for i in range(copies_ref.shape[0]):
        copies_ref[i] = new


def factors(new_ref, rank):
    parts = []
    for i in range(new_ref.shape[0]):
        parts += [new_ref[i], pltpu.roll(new_ref[i], rank, 1)]
    new = jnp.transpose(jnp.concatenate(parts, axis=0))[:rank]
    gram = lax.dot_general(
        new,
        new,
        (((1,), (1,)), ((), ())),
        precision=lax.Precision.HIGHEST,
        preferred_element_type=jnp.float32,
    )
    return jnp.concatenate(split(new), axis=0), jnp.concatenate(split(gram), axis=0)


def raised_part(new, gram, data_ref, own_ref, row, columns):
    rank = new.shape[0] // 2

    def product(left, right):
        high, low = split(right)
        both = jnp.dot(left, high, preferred_element_type=jnp.float32)
        both = both + jnp.dot(left, low, preferred_element_type=jnp.float32)
        return both[:rank] + both[rank:]

    shares = data_ref.shape[0]
    data = jnp.concatenate([data_ref[i, row, :, columns] for i in range(shares)], axis=0)
    own = own_ref[row, :, columns]
    factor = own[:rank]
    raised = factor * product(new, data) / (product(gram, factor) + epsilon)
    return jnp.concatenate([raised, own[rank:]], axis=0)


def border_kernel(
    place_ref, new_ref, data_ref, own_ref, piece_ref, corner_ref, all_new_ref, gram_ref
):
    height, col_count = piece_ref.shape
    row_count = data_ref.shape[0] * (own_ref.shape[0] - 1)
    new, gram = factors(new_ref, height - TILE)
    all_new_ref[...] = new
    gram_ref[...] = gram
    piece_ref[...] = raised_part(new, gram, data_ref, own_ref, own_ref.shape[0] - 1, slice(None))
    place = place_ref[0]
    lowest = (place == data_ref.shape[0] - 1).astype(jnp.int32)
    tile = pl.ds(pl.multiple_of(lowest * (col_count - LANES), LANES), LANES)
    lane = lax.broadcasted_iota(jnp.int32, corner_ref.shape, 1)
    corner = jnp.zeros(corner_ref.shape, jnp.float32)
    for i in range(SMOOTH):
        value = raised_part(new, gram, data_ref, own_ref, i + lowest, tile)
        at = 3 * (i + lowest * (row_count - SMOOTH))
        shift = lax.rem(at + 3 * lowest + 2 * LANES, LANES)
        corner = jnp.where((lane >= at) & (lane < at + 3), pltpu.roll(value, shift, 1), corner)
    side = (place == FIRST) | (place == LAST)
    corner_ref[...] = jnp.where(side, piece_ref[:, :LANES], corner)


def raise_kernel(new_ref, gram_ref, data_ref, own_ref, raised_ref):
    rank = raised_ref.shape[1]
    new, gram = new_ref[...], gram_ref[...]
    for row in range(raised_ref.shape[0]):
        raised_ref[row] = raised_part(new, gram, data_ref, own_ref, row, slice(None))[:rank]


def join_kernel(straight_ref, corner_ref, raised_ref, parts_ref):
    shares, _, share, _ = parts_ref.shape
    strip = raised_ref.shape[0]
    marks = slice(shares * share, shares * share + TILE)
    for i in range(shares):
        ranks = slice(i * share, (i + 1) * share)
        for row in range(strip):
            parts_ref[i, row] = raised_ref[row, ranks]
        parts_ref[i, strip] = straight_ref[ranks]
        parts_ref[i, strip + 1] = straight_ref[marks]
        parts_ref[i, strip + 2, :, :LANES] = corner_ref[ranks]
        parts_ref[i, strip + 2, :, LANES:] = corner_ref[marks]


def side_of(left, right, at):
    lane = lax.broadcasted_iota(jnp.int32, left.shape, 1)
    left = pltpu.roll(left, (LANES - 3 - at) % LANES, 1)
    right = pltpu.roll(right, (LANES - at) % LANES, 1)
    return jnp.where(lane >= LANES - 3, left, jnp.where(lane < 3, right, 0.0))


def smooth_kernel(labels_ref, parts_ref, copies_ref, first, second, marks_ref, weights_ref, done_ref, written):
    share, row_count, col_count = done_ref.shape
    width = first.shape[2]
    strip = parts_ref.shape[1] - 3
    tall = row_count + 2 * SMOOTH
    marks_ref[...] = jnp.zeros(marks_ref.shape, jnp.float32)

    def tiles(place, row):
        if row == strip:
            return parts_ref[place, row, :, :LANES], parts_ref[place, row + 1, :, :LANES]
        return parts_ref[place, row, :, :LANES], parts_ref[place, row, :, LANES:]

    for row in range(tall):
        inner = row - SMOOTH
        if 0 <= inner < row_count:
            main = parts_ref[inner // strip, inner % strip]
            marks = (labels_ref[inner : inner + 1, :] + 1).astype(jnp.float32)
            left, right = tiles(LAST, strip), tiles(FIRST, strip)
        else:
            piece = UPPER[row] if inner < 0 else LOWER[inner - row_count]
            main, marks = parts_ref[piece, strip], parts_ref[piece, strip + 1][:1]
            places = (parts_ref.shape[0] - 1, FIRST) if inner < 0 else (LAST, 0)
            left, right = (tiles(place, strip + 2) for place in places)
        at = 3 * (inner % row_count)
        first[row, :, :col_count] = main
        first[row, :, col_count:] = side_of(left[0], right[0], at)
        marks_ref[row : row + 1, :col_count] = marks
        marks_ref[row : row + 1, col_count:] = side_of(left[1], right[1], at)[:1]
    marks = marks_ref[...]
    total = jnp.ones(marks.shape, jnp.float32)
    found = []
    for shift, axis in ((1, 0), (marks.shape[0] - 1, 0), (1, 1), (width - 1, 1)):
        neighbour = pltpu.roll(marks, shift, axis)
        weight = jnp.where(neighbour == marks, 1.0, 0.25)
        weight = jnp.where(neighbour == 0.0, 0.0, weight)
        found.append(weight)
        total = total + weight
    inverse = 1.0 / total
    weights_ref[0] = inverse
    for i, weight in enumerate(found):
        weights_ref[1 + i] = weight * inverse

    def smoothed(source, row):
        def weight(i):
            return weights_ref[i, row : row + 1, :]

        field = source[row]
        value = weight(0) * field + weight(1) * source[row - 1] + weight(2) * source[row + 1]
        value = value + weight(3) * pltpu.roll(field, 1, 1)
        return value + weight(4) * pltpu.roll(field, width - 1, 1)

    source, target = first, second
    for step in range(1, SMOOTH):
        for row in range(step, tall - step):
            target[row] = smoothed(source, row)
        source, target = target, source
    for top in range(0, row_count, 8):
        rows = [smoothed(source, top + SMOOTH + i)[None, :, :col_count] for i in range(8)]
        done_ref[:, top : top + 8, :] = jnp.swapaxes(jnp.concatenate(rows, axis=0), 0, 1)
    moves = [
        pltpu.make_async_copy(done_ref, copies_ref.at[pl.ds(i * share, share)], written.at[i])
        for i in range(parts_ref.shape[0])
    ]
    for move in moves:
        move.start()
    for move in moves:
        move.wait()


def border_moves(axes, count_ch):
    rows, cols = axes

    def moves(steps):
        pairs = []
        for row in range(rows):
            for col in range(cols):
                for ch, (down, across) in steps.items():
                    if 0 <= row + down < rows and 0 <= col + across < cols:
                        source = (row * cols + col) * count_ch + ch
                        target = ((row + down) * cols + col + across) * count_ch + ch
                        pairs.append((source, target))
        return pairs

    straight = dict.fromkeys(UPPER, (1, 0)) | dict.fromkeys(LOWER, (-1, 0))
    straight |= {LAST: (0, 1), FIRST: (0, -1)}
    corners = {count_ch - 1: (1, 1), FIRST: (1, -1), LAST: (-1, 1), 0: (-1, -1)}
    return moves(straight), moves(corners)


def shards(spectra, pixel_factor, channel_factor, labels):
    rank, row_count, col_count = pixel_factor.shape
    channels = spectra.shape[0]
    shares = lax.axis_size("ch")
    place = lax.axis_index("ch")
    pixels = row_count * col_count
    strip = row_count // shares + 1

    f32 = jnp.float32
    place = place.reshape(1)
    send = (shares, strip, channels, col_count)
    send = kernel_call(
        strips_kernel,
        jax.ShapeDtypeStruct(send, f32),
        scratch_shapes=[
            pltpu.VMEM((row_count // 8, channels, 8, col_count), f32),
            pltpu.VMEM(send, f32),
            pltpu.SemaphoreType.DMA((row_count // 8,)),
            pltpu.SemaphoreType.DMA((row_count // 8 + 1,)),
        ],
        waits=1,
        apart=send,
        operands=(spectra,),
        limit=FIRST_LIMIT,
    )
    sums = kernel_call(
        gram_kernel,
        jax.ShapeDtypeStruct(((rank + channels) // 2, 2 * rank), f32),
        scratch_shapes=[
            pltpu.VMEM((4 * rank, pixels), jnp.bfloat16),
            pltpu.VMEM((2 * rank, pixels), jnp.bfloat16),
        ],
        operands=(spectra, pixel_factor),
        flops=16 * rank * rank * pixels,
    )
    own = kernel_call(
        own_kernel,
        jax.ShapeDtypeStruct((strip, rank + TILE, col_count), f32),
        scratch_shapes=[pltpu.VMEM((shares, strip, rank + TILE, col_count), f32)],
        smem=1,
        operands=(place, pixel_factor, labels),
    )
    data = lax.all_to_all(send, "ch", 0, 0, tiled=True)
    sums = four_sum(pair_sum(sums, "row", 1), "row", 2, 4)
    sums = pair_sum(pair_sum(sums, "col", 1), "col", 2)
    new_channel, copies = kernel_call(
        channel_kernel,
        (
            jax.ShapeDtypeStruct((channels, rank), f32),
            jax.ShapeDtypeStruct((shares, channels // 2, 2 * rank), f32),
        ),
        waits=2,
        operands=(sums, channel_factor.T, data, own),
    )
    copies = lax.all_to_all(copies, "ch", 0, 0, tiled=True)
    flops = 8 * rank * (rank + channels * shares) * col_count
    piece, corner, all_new, gram = kernel_call(
        border_kernel,
        (
            jax.ShapeDtypeStruct((rank + TILE, col_count), f32),
            jax.ShapeDtypeStruct((rank + TILE, LANES), f32),
            jax.ShapeDtypeStruct((2 * rank, shares * channels), jnp.bfloat16),
            jax.ShapeDtypeStruct((2 * rank, rank), jnp.bfloat16),
        ),
        smem=1,
        operands=(place, copies, data, own),
        flops=flops,
    )
    raised = kernel_call(
        raise_kernel,
        jax.ShapeDtypeStruct((strip - 1, rank, col_count), f32),
        operands=(all_new, gram, data, own),
        flops=4 * flops,
    )
    axes = (lax.axis_size("row"), lax.axis_size("col"))
    straight, corners = border_moves(axes, shares)
    everywhere = ("row", "col", "ch")
    straight = lax.ppermute(piece, everywhere, straight)
    corner = lax.ppermute(corner, everywhere, corners)
    share = rank // shares
    parts = kernel_call(
        join_kernel,
        jax.ShapeDtypeStruct((shares, strip + 2, share, col_count), f32),
        operands=(straight, corner, raised),
    )
    parts = lax.all_to_all(parts, "ch", 0, 0, tiled=True)
    tall = row_count + 2 * SMOOTH
    width = col_count + LANES
    field = (rank, row_count, col_count)
    field = kernel_call(
        smooth_kernel,
        jax.ShapeDtypeStruct(field, f32),
        scratch_shapes=[
            pltpu.VMEM((tall, share, width), f32),
            pltpu.VMEM((tall, share, width), f32),
            pltpu.VMEM((tall + -tall % TILE, width), f32),
            pltpu.VMEM((5, tall + -tall % TILE, width), f32),
            pltpu.VMEM((share, row_count, col_count), f32),
            pltpu.SemaphoreType.DMA((shares,)),
        ],
        apart=field,
        operands=(labels, parts),
    )
    field = lax.all_to_all(field, "ch", 0, 0, tiled=True)
    return (field, new_channel.T)


def solution(mesh):
    placed = (P("ch", "row", "col"), P(None, "row", "col"), P(None, "ch"), P("row", "col"))
    return jax.shard_map(
        shards,
        mesh=mesh,
        in_specs=placed,
        out_specs=(P(None, "row", "col"), P(None, "ch")),
        check_vma=False,
    )
```

```python
import jax
import jax.numpy as jnp
from jax import lax
from jax.experimental import pallas as pl
from jax.experimental.pallas import tpu as pltpu
from jax.sharding import PartitionSpec as P

SMOOTH = 3
LANES = 128
TILE = 8
UPPER = (0, 1, 2)
LOWER = (3, 4, 7)
FIRST, LAST = 5, 6
epsilon = 1e-09
VMEM_LIMIT = 48 * 1024 * 1024
FIRST_LIMIT = 62 * 1024 * 1024


def pair_sum(value, axis, distance):
    count = lax.axis_size(axis)
    return value + lax.ppermute(value, axis, [(i, i ^ distance) for i in range(count)])


def four_sum(value, axis, near, far):
    count = lax.axis_size(axis)
    farthest, middle, close = (
        lax.ppermute(value, axis, [(i, i ^ distance) for i in range(count)])
        for distance in (near + far, far, near)
    )
    return (value + close) + (middle + farthest)


def copies_of_all(value, axis):
    count = lax.axis_size(axis)
    copies = jnp.broadcast_to(value[None], (count,) + value.shape)
    return lax.all_to_all(copies, axis, 0, 0, tiled=True)


def kernel_call(
    kernel, out_shape, scratch_shapes=(), smem=0, waits=0, apart=None, operands=(), flops=0, limit=VMEM_LIMIT
):
    traffic = sum(x.size * 4 for x in operands) + sum(x.size * 4 for x in jax.tree.leaves(out_shape))
    in_specs = [
        pl.BlockSpec(memory_space=pltpu.SMEM if i < smem else pltpu.VMEM)
        for i in range(len(operands) - waits)
    ]
    in_specs += [pl.BlockSpec(memory_space=pl.ANY)] * waits
    return pl.pallas_call(
        kernel,
        out_shape=out_shape,
        in_specs=in_specs,
        out_specs=jax.tree.map(
            lambda x: pl.BlockSpec(memory_space=pl.ANY if x.shape == apart else pltpu.VMEM), out_shape
        ),
        scratch_shapes=scratch_shapes,
        compiler_params=pltpu.CompilerParams(vmem_limit_bytes=limit),
        cost_estimate=pl.CostEstimate(flops=flops, bytes_accessed=traffic, transcendentals=0),
    )(*operands)


def split(value):
    high = value.astype(jnp.bfloat16)
    low = (value - high.astype(jnp.float32)).astype(jnp.bfloat16)
    return high, low


def side_pieces(value, row, sides):
    lane = lax.broadcasted_iota(jnp.int32, (value.shape[0], LANES), 1)
    here = (lane >= 3 * row) & (lane < 3 * row + 3)
    last = pltpu.roll(value[:, value.shape[1] - LANES :], 3 * row + 3, 1)
    first = pltpu.roll(value[:, :LANES], 3 * row, 1)
    return jnp.where(here, last, sides[0]), jnp.where(here, first, sides[1])


def strips_kernel(data_ref, send_ref, taken, held, arrived, written):
    channels, row_count, col_count = data_ref.shape
    groups = row_count // 8
    reads = [
        pltpu.make_async_copy(data_ref.at[:, pl.ds(8 * i, 8)], taken.at[i], arrived.at[i])
        for i in range(groups)
    ]
    writes = [
        pltpu.make_async_copy(
            held.at[pl.ds(2 * i, 2), pl.ds(0, 4)], send_ref.at[pl.ds(2 * i, 2), pl.ds(0, 4)], written.at[i]
        )
        for i in range(groups)
    ]
    writes.append(
        pltpu.make_async_copy(
            held.at[:, pl.ds(4, 1)], send_ref.at[:, pl.ds(4, 1)], written.at[groups]
        )
    )
    for read in reads:
        read.start()
    sides = (jnp.zeros((channels, LANES), jnp.float32),) * 2
    for row in range(row_count):
        if row % 8 == 0:
            reads[row // 8].wait()
            eight = jnp.swapaxes(taken[row // 8], 0, 1)
        data = eight[row % 8]
        held[row // 4, row % 4] = data
        if row >= row_count - SMOOTH:
            held[UPPER[row - row_count + SMOOTH], 4] = data
        if row < SMOOTH:
            held[LOWER[row], 4] = data
        sides = side_pieces(data, row, sides)
        if row % 8 == 7:
            writes[row // 8].start()
    for i, place in enumerate((LAST, FIRST)):
        held[place, 4, :, :LANES] = sides[i]
        held[place, 4, :, LANES:] = jnp.zeros((channels, col_count - LANES), jnp.float32)
    writes[groups].start()
    for write in writes:
        write.wait()


def gram_kernel(data_ref, factor_ref, sums_ref, wide, tall):
    channels = data_ref.shape[0]
    rank, row_count, col_count = factor_ref.shape
    both = rank + channels
    half = 2 * rank
    for top in (both, half + both):
        wide[top : top + half - both] = jnp.zeros((half - both, wide.shape[1]), jnp.bfloat16)
    for row in range(row_count):
        if row % 8 == 0:
            data = jnp.swapaxes(data_ref[:, row : row + 8, :], 0, 1)
            factor = jnp.swapaxes(factor_ref[:, row : row + 8, :], 0, 1)
        high, low = split(jnp.concatenate([factor[row % 8], data[row % 8]], axis=0))
        columns = slice(row * col_count, (row + 1) * col_count)
        wide[0:both, columns] = high
        wide[half : half + both, columns] = low
        tall[0:rank, columns] = high[:rank]
        tall[rank:half, columns] = low[:rank]
    products = lax.dot_general(
        wide[...], tall[...], (((1,), (1,)), ((), ())), preferred_element_type=jnp.float32
    )
    products = products[0:half] + products[half:]
    products = products + pltpu.roll(products, rank, 1)
    packed = both // 2
    lane = lax.broadcasted_iota(jnp.int32, (packed, LANES), 1)
    sums_ref[...] = jnp.where(lane < rank, products[0:packed], products[packed:both])


def own_kernel(place_ref, factor_ref, labels_ref, own_ref, rows_ref):
    rank, row_count, col_count = factor_ref.shape
    sides = (jnp.zeros((rank + TILE, LANES), jnp.float32),) * 2
    for row in range(row_count):
        if row % 8 == 0:
            eight = jnp.swapaxes(factor_ref[:, row : row + 8, :], 0, 1)
        marks = (labels_ref[row : row + 1, :] + 1).astype(jnp.float32)
        marks = jnp.broadcast_to(marks, (TILE, col_count))
        marked = jnp.concatenate([eight[row % 8], marks], axis=0)
        rows_ref[row // 4, row % 4] = marked
        if row >= row_count - SMOOTH:
            rows_ref[UPPER[row - row_count + SMOOTH], 4] = marked
        if row < SMOOTH:
            rows_ref[LOWER[row], 4] = marked
        sides = side_pieces(marked, row, sides)
    for i, place in enumerate((LAST, FIRST)):
        rows_ref[place, 4, :, :LANES] = sides[i]
        rows_ref[place, 4, :, LANES:] = jnp.zeros((rank + TILE, col_count - LANES), jnp.float32)
    own_ref[...] = rows_ref[place_ref[0]]


def channel_kernel(sums_ref, factor_ref, data_ref, own_ref, new_ref, copies_ref):
    channels, rank = factor_ref.shape
    total = sums_ref[...]
    total = jnp.concatenate([total, pltpu.roll(total, rank, 1)], axis=0)[:, :rank]
    gram, top = total[:rank], total[rank:]
    factor = factor_ref[...]
    lower = lax.dot_general(
        factor,
        gram,
        (((1,), (1,)), ((), ())),
        precision=lax.Precision.HIGHEST,
        preferred_element_type=jnp.float32,
    )
    new = factor * top / (lower + epsilon)
    new_ref[...] = new
    packed = channels // 2
    new = jnp.concatenate([new[:packed], new[packed:]], axis=1)
    for i in range(copies_ref.shape[0]):
        copies_ref[i] = new


def factors(new_ref, rank):
    parts = []
    for i in range(new_ref.shape[0]):
        parts += [new_ref[i], pltpu.roll(new_ref[i], rank, 1)]
    new = jnp.transpose(jnp.concatenate(parts, axis=0))[:rank]
    gram = lax.dot_general(
        new,
        new,
        (((1,), (1,)), ((), ())),
        precision=lax.Precision.HIGHEST,
        preferred_element_type=jnp.float32,
    )
    return jnp.concatenate(split(new), axis=0), jnp.concatenate(split(gram), axis=0)


def raised_part(new, gram, data_ref, own_ref, row, columns):
    rank = new.shape[0] // 2

    def product(left, right):
        high, low = split(right)
        both = jnp.dot(left, high, preferred_element_type=jnp.float32)
        both = both + jnp.dot(left, low, preferred_element_type=jnp.float32)
        return both[:rank] + both[rank:]

    shares = data_ref.shape[0]
    data = jnp.concatenate([data_ref[i, row, :, columns] for i in range(shares)], axis=0)
    own = own_ref[row, :, columns]
    factor = own[:rank]
    raised = factor * product(new, data) / (product(gram, factor) + epsilon)
    return jnp.concatenate([raised, own[rank:]], axis=0)


def border_kernel(
    place_ref, new_ref, data_ref, own_ref, piece_ref, corner_ref, all_new_ref, gram_ref
):
    height, col_count = piece_ref.shape
    row_count = data_ref.shape[0] * (own_ref.shape[0] - 1)
    new, gram = factors(new_ref, height - TILE)
    all_new_ref[...] = new
    gram_ref[...] = gram
    piece_ref[...] = raised_part(new, gram, data_ref, own_ref, own_ref.shape[0] - 1, slice(None))
    place = place_ref[0]
    lowest = (place == data_ref.shape[0] - 1).astype(jnp.int32)
    tile = pl.ds(pl.multiple_of(lowest * (col_count - LANES), LANES), LANES)
    lane = lax.broadcasted_iota(jnp.int32, corner_ref.shape, 1)
    corner = jnp.zeros(corner_ref.shape, jnp.float32)
    for i in range(SMOOTH):
        value = raised_part(new, gram, data_ref, own_ref, i + lowest, tile)
        at = 3 * (i + lowest * (row_count - SMOOTH))
        shift = lax.rem(at + 3 * lowest + 2 * LANES, LANES)
        corner = jnp.where((lane >= at) & (lane < at + 3), pltpu.roll(value, shift, 1), corner)
    side = (place == FIRST) | (place == LAST)
    corner_ref[...] = jnp.where(side, piece_ref[:, :LANES], corner)


def raise_kernel(new_ref, gram_ref, data_ref, own_ref, raised_ref):
    rank = raised_ref.shape[1]
    new, gram = new_ref[...], gram_ref[...]
    for row in range(raised_ref.shape[0]):
        raised_ref[row] = raised_part(new, gram, data_ref, own_ref, row, slice(None))[:rank]


def join_kernel(straight_ref, corner_ref, raised_ref, parts_ref):
    shares, _, share, _ = parts_ref.shape
    strip = raised_ref.shape[0]
    marks = slice(shares * share, shares * share + TILE)
    for i in range(shares):
        ranks = slice(i * share, (i + 1) * share)
        for row in range(strip):
            parts_ref[i, row] = raised_ref[row, ranks]
        parts_ref[i, strip] = straight_ref[ranks]
        parts_ref[i, strip + 1] = straight_ref[marks]
        parts_ref[i, strip + 2, :, :LANES] = corner_ref[ranks]
        parts_ref[i, strip + 2, :, LANES:] = corner_ref[marks]


def side_of(left, right, at):
    lane = lax.broadcasted_iota(jnp.int32, left.shape, 1)
    left = pltpu.roll(left, (LANES - 3 - at) % LANES, 1)
    right = pltpu.roll(right, (LANES - at) % LANES, 1)
    return jnp.where(lane >= LANES - 3, left, jnp.where(lane < 3, right, 0.0))


def smooth_kernel(labels_ref, parts_ref, copies_ref, first, second, marks_ref, weights_ref, done_ref, written):
    share, row_count, col_count = done_ref.shape
    width = first.shape[2]
    strip = parts_ref.shape[1] - 3
    tall = row_count + 2 * SMOOTH
    marks_ref[...] = jnp.zeros(marks_ref.shape, jnp.float32)

    def tiles(place, row):
        if row == strip:
            return parts_ref[place, row, :, :LANES], parts_ref[place, row + 1, :, :LANES]
        return parts_ref[place, row, :, :LANES], parts_ref[place, row, :, LANES:]

    for row in range(tall):
        inner = row - SMOOTH
        if 0 <= inner < row_count:
            main = parts_ref[inner // strip, inner % strip]
            marks = (labels_ref[inner : inner + 1, :] + 1).astype(jnp.float32)
            left, right = tiles(LAST, strip), tiles(FIRST, strip)
        else:
            piece = UPPER[row] if inner < 0 else LOWER[inner - row_count]
            main, marks = parts_ref[piece, strip], parts_ref[piece, strip + 1][:1]
            places = (parts_ref.shape[0] - 1, FIRST) if inner < 0 else (LAST, 0)
            left, right = (tiles(place, strip + 2) for place in places)
        at = 3 * (inner % row_count)
        first[row, :, :col_count] = main
        first[row, :, col_count:] = side_of(left[0], right[0], at)
        marks_ref[row : row + 1, :col_count] = marks
        marks_ref[row : row + 1, col_count:] = side_of(left[1], right[1], at)[:1]
    marks = marks_ref[...]
    total = jnp.ones(marks.shape, jnp.float32)
    found = []
    for shift, axis in ((1, 0), (marks.shape[0] - 1, 0), (1, 1), (width - 1, 1)):
        neighbour = pltpu.roll(marks, shift, axis)
        weight = jnp.where(neighbour == marks, 1.0, 0.25)
        weight = jnp.where(neighbour == 0.0, 0.0, weight)
        found.append(weight)
        total = total + weight
    inverse = 1.0 / total
    weights_ref[0] = inverse
    for i, weight in enumerate(found):
        weights_ref[1 + i] = weight * inverse

    def smoothed(source, row):
        def weight(i):
            return weights_ref[i, row : row + 1, :]

        field = source[row]
        value = weight(0) * field + weight(1) * source[row - 1] + weight(2) * source[row + 1]
        value = value + weight(3) * pltpu.roll(field, 1, 1)
        return value + weight(4) * pltpu.roll(field, width - 1, 1)

    source, target = first, second
    for step in range(1, SMOOTH):
        for row in range(step, tall - step):
            target[row] = smoothed(source, row)
        source, target = target, source
    moves = []
    for top in range(0, row_count, 8):
        rows = [smoothed(source, top + SMOOTH + i)[None, :, :col_count] for i in range(8)]
        done_ref[:, top : top + 8, :] = jnp.swapaxes(jnp.concatenate(rows, axis=0), 0, 1)
        for i in range(copies_ref.shape[0] // share):
            target = copies_ref.at[pl.ds(i * share, share), pl.ds(top, 8)]
            moves.append(
                pltpu.make_async_copy(done_ref.at[:, pl.ds(top, 8)], target, written.at[len(moves)])
            )
            moves[-1].start()
    for move in moves:
        move.wait()


def border_moves(axes, count_ch):
    rows, cols = axes

    def moves(steps):
        pairs = []
        for row in range(rows):
            for col in range(cols):
                for ch, (down, across) in steps.items():
                    if 0 <= row + down < rows and 0 <= col + across < cols:
                        source = (row * cols + col) * count_ch + ch
                        target = ((row + down) * cols + col + across) * count_ch + ch
                        pairs.append((source, target))
        return pairs

    straight = dict.fromkeys(UPPER, (1, 0)) | dict.fromkeys(LOWER, (-1, 0))
    straight |= {LAST: (0, 1), FIRST: (0, -1)}
    corners = {count_ch - 1: (1, 1), FIRST: (1, -1), LAST: (-1, 1), 0: (-1, -1)}
    return moves(straight), moves(corners)


def shards(spectra, pixel_factor, channel_factor, labels):
    rank, row_count, col_count = pixel_factor.shape
    channels = spectra.shape[0]
    shares = lax.axis_size("ch")
    place = lax.axis_index("ch")
    pixels = row_count * col_count
    strip = row_count // shares + 1

    f32 = jnp.float32
    place = place.reshape(1)
    send = (shares, strip, channels, col_count)
    send = kernel_call(
        strips_kernel,
        jax.ShapeDtypeStruct(send, f32),
        scratch_shapes=[
            pltpu.VMEM((row_count // 8, channels, 8, col_count), f32),
            pltpu.VMEM(send, f32),
            pltpu.SemaphoreType.DMA((row_count // 8,)),
            pltpu.SemaphoreType.DMA((row_count // 8 + 1,)),
        ],
        waits=1,
        apart=send,
        operands=(spectra,),
        limit=FIRST_LIMIT,
    )
    sums = kernel_call(
        gram_kernel,
        jax.ShapeDtypeStruct(((rank + channels) // 2, 2 * rank), f32),
        scratch_shapes=[
            pltpu.VMEM((4 * rank, pixels), jnp.bfloat16),
            pltpu.VMEM((2 * rank, pixels), jnp.bfloat16),
        ],
        operands=(spectra, pixel_factor),
        flops=16 * rank * rank * pixels,
    )
    own = kernel_call(
        own_kernel,
        jax.ShapeDtypeStruct((strip, rank + TILE, col_count), f32),
        scratch_shapes=[pltpu.VMEM((shares, strip, rank + TILE, col_count), f32)],
        smem=1,
        operands=(place, pixel_factor, labels),
    )
    data = lax.all_to_all(send, "ch", 0, 0, tiled=True)
    sums = four_sum(pair_sum(sums, "row", 1), "row", 2, 4)
    sums = pair_sum(pair_sum(sums, "col", 1), "col", 2)
    new_channel, copies = kernel_call(
        channel_kernel,
        (
            jax.ShapeDtypeStruct((channels, rank), f32),
            jax.ShapeDtypeStruct((shares, channels // 2, 2 * rank), f32),
        ),
        waits=2,
        operands=(sums, channel_factor.T, data, own),
    )
    copies = lax.all_to_all(copies, "ch", 0, 0, tiled=True)
    flops = 8 * rank * (rank + channels * shares) * col_count
    piece, corner, all_new, gram = kernel_call(
        border_kernel,
        (
            jax.ShapeDtypeStruct((rank + TILE, col_count), f32),
            jax.ShapeDtypeStruct((rank + TILE, LANES), f32),
            jax.ShapeDtypeStruct((2 * rank, shares * channels), jnp.bfloat16),
            jax.ShapeDtypeStruct((2 * rank, rank), jnp.bfloat16),
        ),
        smem=1,
        operands=(place, copies, data, own),
        flops=flops,
    )
    raised = kernel_call(
        raise_kernel,
        jax.ShapeDtypeStruct((strip - 1, rank, col_count), f32),
        operands=(all_new, gram, data, own),
        flops=4 * flops,
    )
    axes = (lax.axis_size("row"), lax.axis_size("col"))
    straight, corners = border_moves(axes, shares)
    everywhere = ("row", "col", "ch")
    straight = lax.ppermute(piece, everywhere, straight)
    corner = lax.ppermute(corner, everywhere, corners)
    share = rank // shares
    parts = kernel_call(
        join_kernel,
        jax.ShapeDtypeStruct((shares, strip + 2, share, col_count), f32),
        operands=(straight, corner, raised),
    )
    parts = lax.all_to_all(parts, "ch", 0, 0, tiled=True)
    tall = row_count + 2 * SMOOTH
    width = col_count + LANES
    field = (rank, row_count, col_count)
    field = kernel_call(
        smooth_kernel,
        jax.ShapeDtypeStruct(field, f32),
        scratch_shapes=[
            pltpu.VMEM((tall, share, width), f32),
            pltpu.VMEM((tall, share, width), f32),
            pltpu.VMEM((tall + -tall % TILE, width), f32),
            pltpu.VMEM((5, tall + -tall % TILE, width), f32),
            pltpu.VMEM((share, row_count, col_count), f32),
            pltpu.SemaphoreType.DMA((shares * row_count // 8,)),
        ],
        apart=field,
        operands=(labels, parts),
    )
    field = lax.all_to_all(field, "ch", 0, 0, tiled=True)
    return (field, new_channel.T)


def solution(mesh):
    placed = (P("ch", "row", "col"), P(None, "row", "col"), P(None, "ch"), P("row", "col"))
    return jax.shard_map(
        shards,
        mesh=mesh,
        in_specs=placed,
        out_specs=(P(None, "row", "col"), P(None, "ch")),
        check_vma=False,
    )
```
